256 devices in a mesh: ctx: 64 (over z, x, core), tp: 4 (over y).
Axes of the slice: x: 4, y: 4, z: 8, core: 2. Of those that a mesh axis runs over, the one named last changes fastest.
Arguments:
- queries: bfloat16 [32768, 12, 192], P('ctx', 'tp'), may hold values from -8 to 8
- key_rows: bfloat16 [32768, 192], P('ctx'), may hold values from -8 to 8
- values: bfloat16 [32768, 192], P('ctx'), may hold values from -6 to 6
- grad_out: bfloat16 [32768, 12, 192], P('ctx', 'tp'), may hold values from -6 to 6
- doc_ids: int32 [32768], P('ctx'), may hold values from 0 to 31, never falling along the last dimension, each value on 1 to 2048 neighbouring positions
Outputs:
- attended: bfloat16 [32768, 12, 192], P('ctx', 'tp')
- grad_queries: bfloat16 [32768, 12, 192], P('ctx', 'tp')
- grad_keys: bfloat16 [32768, 192], P(('ctx', 'tp'))
- grad_values: bfloat16 [32768, 192], P(('ctx', 'tp'))
The draws below stay inside these ranges and needn't reach their ends.
Inputs may be any that keep to these rules, and one draw needn't show every extreme that they name: `doc_ids`: document numbers never fall along the sequence; each document holds 1 to 2048 consecutive tokens, and one holds exactly 2048.
All inputs are finite; a program needn't handle non-finite values.
Results may differ from the reference program's by a relative error of at most 0.018.
Values may be sent and summed in bfloat16 or wider, within the bound.
No kernel may reach another device: no remote copies, remote signals or barrier semaphores. Data moves between devices by JAX's collectives and lax.ppermute only.
A program may use at most 64 MiB of HBM per device.

```python
import math
import jax
import jax.numpy as jnp
import numpy as np
from jax import lax

HEADS = 12
HEAD_DIM = 192
TOK_DEV = 512
LOOKBACK = 4
MAXDOC = 2048
DOCS = 32
TOKENS = 32768
N_CTX = 64


def draw_key_rows(key, part):
    key = jax.random.fold_in(key, 11)
    return jnp.clip(1.5 * jax.random.normal(key, (TOKENS, HEAD_DIM), jnp.float32), -6.0, 6.0).astype(jnp.bfloat16)


def draw_queries(key, part):
    key = jax.random.fold_in(key, 12)
    return jnp.clip(1.5 * jax.random.normal(key, (TOKENS, HEADS, HEAD_DIM), jnp.float32), -6.0, 6.0).astype(jnp.bfloat16)


def steps_of(key, dims, split, least, top_value):
    level, own = 1.0, jax.random.fold_in(key, 6)
    for position, shards_of in split:
        draws = jnp.exp(jax.random.uniform(jax.random.fold_in(own, position), (shards_of,), jnp.float32, least / len(split), top_value / len(split)))
        level = level * jnp.repeat(draws, dims[position] // shards_of).reshape([-1 if axis == position else 1 for axis in range(len(dims))])
    return level


def profile(amount, total, limit, skew):
    weights = [(1 << 20) // math.isqrt(rank ** skew) + 1 for rank in range(2, amount + 1)]
    rest, given = total - limit - (amount - 1), [1] * (amount - 1)
    while rest > 0:
        free = [i for i in range(amount - 1) if given[i] < limit]
        whole, remaining = sum([weights[i] for i in free]), rest
        for i in free:
            addition = min(limit - given[i], max(1, remaining * weights[i] // whole), rest)
            given[i] = given[i] + addition
            rest = rest - addition
    return np.array([limit] + given)


def ragged_sizes(key, count, total, bound, slope):
    if count == 2:
        one = jax.random.randint(key, (), max(1, total - bound), min(bound, total - 1) + 1)
        return jnp.stack([one, total - one])
    tallies = jnp.asarray(profile(count, total, bound, slope), jnp.int32)
    pairs = (count - 1) // 2
    giver, receiver = tallies[1:1 + 2 * pairs:2], tallies[2:2 + 2 * pairs:2]
    margin = jnp.minimum(giver - 1, bound - receiver)
    passed = jax.random.randint(jax.random.fold_in(key, 1), (pairs,), 0, 1 << 20) % (margin + 1)
    tallies = tallies.at[1:1 + 2 * pairs:2].set(giver - passed).at[2:2 + 2 * pairs:2].set(receiver + passed)
    return tallies[jax.random.permutation(jax.random.fold_in(key, 2), count)]


def gaussian(rng, shape, width, reach, cuts=(), kind=jnp.bfloat16):
    gain = steps_of(rng, shape, cuts, -0.22, 0.18) if cuts else 1.0
    array = jax.random.normal(rng, shape, jnp.float32) * width * gain
    return jnp.minimum(jnp.maximum(array, -reach), reach).astype(kind)


def setup_inputs(seed: int = 0) -> dict:
    splits = jax.random.split(jax.random.key(seed), 6)
    return {
        "queries": draw_queries(jax.random.fold_in(splits[5], 71), 0),
        "key_rows": draw_key_rows(jax.random.fold_in(splits[5], 71), 0),
        "values": gaussian(splits[2], (TOKENS, HEAD_DIM), 1.0, 6.0, ((0, 64),)),
        "grad_out": gaussian(splits[3], (TOKENS, HEADS, HEAD_DIM), 1.0, 6.0, ((0, 64), (1, 4))),
        "doc_ids": jnp.searchsorted(jnp.cumsum(ragged_sizes(splits[4], DOCS, TOKENS, MAXDOC, 1)), jnp.arange(TOKENS), side="right").astype(jnp.int32),
    }


NEGATIVE = -1.0e30


def block_terms(query_block, grad_block, key_window, value_window, query_docs, key_docs, query_places, key_places):
    scaling = query_block.shape[-1] ** -0.5
    visible = (query_docs[:, None] == key_docs[None, :]) & (key_places[None, :] <= query_places[:, None])
    scores = jnp.einsum("qhe,ke->hqk", query_block.astype(jnp.float32), key_window.astype(jnp.float32)) * scaling
    scores = jnp.where(visible[None], scores, NEGATIVE)
    highest = jnp.max(scores, axis=-1, keepdims=True)
    exponent = jnp.exp(scores - highest)
    probability = exponent / jnp.sum(exponent, axis=-1, keepdims=True)
    weights = probability.astype(jnp.bfloat16)
    attended = jnp.einsum("hqk,ke->qhe", weights.astype(jnp.float32), value_window.astype(jnp.float32)).astype(jnp.bfloat16)
    row_delta = jnp.sum(grad_block.astype(jnp.float32) * attended.astype(jnp.float32), axis=-1)
    grad_probability = jnp.einsum("qhe,ke->hqk", grad_block.astype(jnp.float32), value_window.astype(jnp.float32))
    grad_scores = (scaling * probability * (grad_probability - jnp.transpose(row_delta)[:, :, None])).astype(jnp.bfloat16)
    grad_queries = jnp.einsum("hqk,ke->qhe", grad_scores.astype(jnp.float32), key_window.astype(jnp.float32)).astype(jnp.bfloat16)
    grad_keys = jnp.einsum("hqk,qhe->ke", grad_scores.astype(jnp.float32), query_block.astype(jnp.float32))
    grad_values = jnp.einsum("hqk,qhe->ke", weights.astype(jnp.float32), grad_block.astype(jnp.float32))
    return attended, grad_queries, grad_keys, grad_values


def reference(queries, key_rows, values, grad_out, doc_ids):
    token_count = queries.shape[0]
    head_dim = key_rows.shape[1]
    span_rows = LOOKBACK * TOK_DEV
    window_len = (LOOKBACK + 1) * TOK_DEV
    key_padded = jnp.concatenate([jnp.zeros((span_rows, head_dim), key_rows.dtype), key_rows], axis=0)
    value_padded = jnp.concatenate([jnp.zeros((span_rows, head_dim), values.dtype), values], axis=0)
    docs_padded = jnp.concatenate([jnp.full((span_rows,), -1, jnp.int32), doc_ids.astype(jnp.int32)], axis=0)

    def block_step(carried, block_index):
        key_grads, value_grads = carried
        first_row = (block_index * TOK_DEV).astype(jnp.int32)
        query_block = lax.dynamic_slice_in_dim(queries, first_row, TOK_DEV, 0)
        grad_block = lax.dynamic_slice_in_dim(grad_out, first_row, TOK_DEV, 0)
        key_window = lax.dynamic_slice_in_dim(key_padded, first_row, window_len, 0)
        value_window = lax.dynamic_slice_in_dim(value_padded, first_row, window_len, 0)
        query_docs = lax.dynamic_slice_in_dim(doc_ids.astype(jnp.int32), first_row, TOK_DEV, 0)
        key_docs = lax.dynamic_slice_in_dim(docs_padded, first_row, window_len, 0)
        query_places = first_row + jnp.arange(TOK_DEV, dtype=jnp.int32)
        key_places = first_row - span_rows + jnp.arange(window_len, dtype=jnp.int32)
        attended, grad_queries, grad_key, grad_value = block_terms(query_block, grad_block, key_window, value_window, query_docs, key_docs, query_places, key_places)
        key_grads = lax.dynamic_update_slice_in_dim(key_grads, lax.dynamic_slice_in_dim(key_grads, first_row, window_len, 0) + grad_key, first_row, 0)
        value_grads = lax.dynamic_update_slice_in_dim(value_grads, lax.dynamic_slice_in_dim(value_grads, first_row, window_len, 0) + grad_value, first_row, 0)
        return (key_grads, value_grads), (attended, grad_queries)

    zero_grads = jnp.zeros((token_count + span_rows, head_dim), jnp.float32)
    carried, stacked = lax.scan(block_step, (zero_grads, zero_grads), jnp.arange(N_CTX, dtype=jnp.int32))
    key_grads, value_grads = carried
    attended = stacked[0].reshape(queries.shape)
    grad_queries = stacked[1].reshape(queries.shape)
    return attended, grad_queries, key_grads[span_rows:].astype(jnp.bfloat16), value_grads[span_rows:].astype(jnp.bfloat16)
```

```python
import jax
import jax.numpy as jnp
from jax import lax
from jax.experimental import pallas as pl
from jax.experimental.pallas import tpu as pltpu
from jax.sharding import PartitionSpec as P

LOG2E = 1.4426950408889634
NEGATIVE = -1e30
ROWS = 512
CHUNK = 256
PIECE = 128
DIM = 192
DOC_ROW = 2 * DIM
PACKED = DOC_ROW + 16
REMOTE_CHUNKS = 8
HEADS = 3
COLS = HEADS * ROWS
OFFSETS = (0, 3, 1, 2)
F32 = jnp.float32
BF16 = jnp.bfloat16


def dot(a, b):
    return jnp.dot(a, b, preferred_element_type=F32)


def one_hot(docs, width):
    rows = lax.broadcasted_iota(jnp.int32, (64, width), 0).astype(F32)
    return rows == docs.astype(F32)


def attention_kernel(
    tp_ref, q_ref, do_ref, own_ref, g0_ref, g1_ref, g2_ref, g3_ref, sw_ref,
    o_ref, dq_ref, dkv_ref,
    kt, vt, kn, vn, scores, weights, ds_ref, qe, qn, dop, don, top, total, oacc, dqacc,
):
    tp = tp_ref[0]
    gathered = (g0_ref, g1_ref, g2_ref, g3_ref)
    scale = DIM ** -0.5
    to_log2 = scale * LOG2E

    def piece_of(tile, slot):
        if tile % 2 == 0:
            return gathered[slot].at[tile // 2]
        return sw_ref.at[slot, tile // 2]

    own_docs = own_ref[DOC_ROW : DOC_ROW + 1, :].astype(F32)
    first_doc = own_docs[:, 0:1]
    matches = jnp.zeros((1, PIECE), F32)
    for tile in range(4):
        for slot in range(4):
            docs = piece_of(tile, slot)[DOC_ROW : DOC_ROW + 1, :].astype(F32)
            matches = matches + jnp.where(docs == first_doc, 1.0, 0.0)
    reach = jnp.sum(matches).astype(jnp.int32)
    first_chunk = (REMOTE_CHUNKS * CHUNK - reach) // CHUNK

    def place(chunk, lanes, rows, piece):
        width = piece.shape[1]
        keys = piece[0:DIM, :]
        vals = piece[DIM : 2 * DIM, :]
        kt[chunk, :, lanes] = keys
        vt[chunk, :, lanes] = vals
        hot = one_hot(piece[DOC_ROW : DOC_ROW + 1, :], width).astype(F32).astype(BF16)
        kn[chunk, rows, :] = jnp.concatenate([keys, hot], axis=0).T
        vn[chunk, rows, :] = vals.T

    for tile in range(4):
        for slot in range(4):
            quarter = lax.rem(tp + OFFSETS[slot], 4)
            chunk = tile * 2 + quarter // 2
            half = lax.rem(quarter, 2) * PIECE

            @pl.when(chunk >= first_chunk)
            def _():
                span = pl.ds(pl.multiple_of(half, PIECE), PIECE)
                place(chunk, span, span, piece_of(tile, slot)[...])

    for part in range(2):
        span = slice(part * CHUNK, (part + 1) * CHUNK)
        place(REMOTE_CHUNKS + part, slice(None), slice(None), own_ref[:, span])

    mask_rows = jnp.where(one_hot(own_docs, ROWS), 0.0, NEGATIVE).astype(BF16)
    for head in range(HEADS):
        cols = slice(head * ROWS, (head + 1) * ROWS)
        qe[0:DIM, cols] = q_ref[head]
        qe[DIM:, cols] = mask_rows
        qn[cols, :] = q_ref[head].T

    causal = lax.broadcasted_iota(jnp.int32, (CHUNK, CHUNK), 0) <= lax.broadcasted_iota(
        jnp.int32, (CHUNK, CHUNK), 1
    )

    def highest(s):
        return jnp.max(s.reshape(CHUNK // 8, 8, s.shape[1]), axis=0)

    for head in range(HEADS):
        low = slice(head * ROWS, head * ROWS + CHUNK)
        high = slice(head * ROWS + CHUNK, (head + 1) * ROWS)
        s_low = jnp.where(causal, dot(kn[REMOTE_CHUNKS], qe[:, low]), NEGATIVE)
        s_high = dot(kn[REMOTE_CHUNKS], qe[:, high])
        s_last = jnp.where(causal, dot(kn[REMOTE_CHUNKS + 1], qe[:, high]), NEGATIVE)
        scores[REMOTE_CHUNKS, :, low] = s_low
        scores[REMOTE_CHUNKS, :, high] = s_high
        scores[REMOTE_CHUNKS + 1, :, high] = s_last
        top[:, low] = highest(s_low)
        top[:, high] = jnp.maximum(highest(s_high), highest(s_last))

    @pl.loop(first_chunk, REMOTE_CHUNKS)
    def _(chunk):
        for head in range(HEADS):
            cols = slice(head * ROWS, (head + 1) * ROWS)
            s = dot(kn[chunk], qe[:, cols])
            scores[chunk, :, cols] = s
            top[:, cols] = jnp.maximum(top[:, cols], highest(s))

    top[...] = jnp.broadcast_to(jnp.max(top[...], axis=0, keepdims=True) * to_log2, (8, COLS))

    def exponent(chunk, cols):
        width = cols.stop - cols.start
        s = scores[chunk, :, cols].reshape(CHUNK // 8, 8, width)
        e = jnp.exp2(s * to_log2 - top[:, cols][None])
        part = jnp.sum(e, axis=0)
        w = e.reshape(CHUNK, width).astype(BF16)
        weights[chunk, :, cols] = w
        return part, w

    for head in range(HEADS):
        cols = slice(head * ROWS, (head + 1) * ROWS)
        high = slice(head * ROWS + CHUNK, (head + 1) * ROWS)
        part, w = exponent(REMOTE_CHUNKS, cols)
        total[:, cols] = part
        oacc[:, cols] = dot(vt[REMOTE_CHUNKS], w)
        part, w = exponent(REMOTE_CHUNKS + 1, high)
        total[:, high] += part
        oacc[:, high] += dot(vt[REMOTE_CHUNKS + 1], w)

    @pl.loop(first_chunk, REMOTE_CHUNKS)
    def _(chunk):
        for head in range(HEADS):
            cols = slice(head * ROWS, (head + 1) * ROWS)
            part, w = exponent(chunk, cols)
            total[:, cols] += part
            oacc[:, cols] += dot(vt[chunk], w)

    for head in range(HEADS):
        cols = slice(head * ROWS, (head + 1) * ROWS)
        inverse = 1.0 / jnp.sum(total[:, cols], axis=0, keepdims=True)
        attended = (oacc[:, cols] * inverse).astype(BF16)
        o_ref[head] = attended
        grads = do_ref[head].astype(F32)
        delta = jnp.sum(grads * attended.astype(F32), axis=0, keepdims=True)
        ratio = inverse * scale
        top[:, cols] = jnp.broadcast_to(delta * ratio, (8, ROWS))
        scaled = (grads * ratio).astype(BF16)
        dop[:, cols] = scaled
        don[cols, :] = scaled.T

    def grad_scores(chunk, cols):
        width = cols.stop - cols.start
        dp = dot(vn[chunk], dop[:, cols]).reshape(CHUNK // 8, 8, width)
        w = weights[chunk, :, cols].astype(F32).reshape(CHUNK // 8, 8, width)
        ds = (w * (dp - top[:, cols][None])).reshape(CHUNK, width).astype(BF16)
        ds_ref[:, cols] = ds
        return ds

    def emit(chunk, dk, dv):
        both = jnp.concatenate([dk, dv * (1.0 / scale)], axis=1).astype(BF16)
        for half in range(2):
            quarter = lax.rem(chunk, 2) * 2 + half
            off = lax.rem(quarter - tp + 4, 4)
            slot = jnp.where(off == 0, 0, jnp.where(off == 3, 1, off + 1))
            dkv_ref[chunk // 2, slot] = both[half * PIECE : (half + 1) * PIECE]

    for part in range(2):
        chunk = REMOTE_CHUNKS + part
        dk = jnp.zeros((CHUNK, DIM), F32)
        dv = jnp.zeros((CHUNK, DIM), F32)
        for head in range(HEADS):
            cols = slice(head * ROWS + part * CHUNK, (head + 1) * ROWS)
            ds = grad_scores(chunk, cols)
            dq = dot(kt[chunk], ds)
            if part == 0:
                dqacc[:, cols] = dq
            else:
                dqacc[:, cols] += dq
            dk = dk + dot(ds, qn[cols, :])
            dv = dv + dot(weights[chunk, :, cols], don[cols, :])
        emit(chunk, dk, dv)

    @pl.loop(first_chunk, REMOTE_CHUNKS)
    def _(chunk):
        for head in range(HEADS):
            cols = slice(head * ROWS, (head + 1) * ROWS)
            ds = grad_scores(chunk, cols)
            dqacc[:, cols] += dot(kt[chunk], ds)
        emit(chunk, dot(ds_ref[...], qn[...]), dot(weights[chunk], don[...]))

    @pl.loop(0, first_chunk)
    def _(chunk):
        emit(chunk, jnp.zeros((CHUNK, DIM), F32), jnp.zeros((CHUNK, DIM), F32))

    for head in range(HEADS):
        dq_ref[head] = dqacc[:, head * ROWS : (head + 1) * ROWS].astype(BF16)


def attend(tp, q, do, own, gathered, swapped):
    vmem = pl.BlockSpec(memory_space=pltpu.VMEM)
    chunks = REMOTE_CHUNKS + 2
    return pl.pallas_call(
        attention_kernel,
        out_shape=(
            jax.ShapeDtypeStruct((HEADS, DIM, ROWS), BF16),
            jax.ShapeDtypeStruct((HEADS, DIM, ROWS), BF16),
            jax.ShapeDtypeStruct((5, 4, PIECE, 2 * DIM), BF16),
        ),
        in_specs=[pl.BlockSpec(memory_space=pltpu.SMEM)] + [vmem] * 8,
        out_specs=(vmem, vmem, vmem),
        scratch_shapes=[
            pltpu.VMEM((chunks, DIM, CHUNK), BF16),
            pltpu.VMEM((chunks, DIM, CHUNK), BF16),
            pltpu.VMEM((chunks, CHUNK, CHUNK), BF16),
            pltpu.VMEM((chunks, CHUNK, DIM), BF16),
            pltpu.VMEM((chunks, CHUNK, COLS), F32),
            pltpu.VMEM((chunks, CHUNK, COLS), BF16),
            pltpu.VMEM((CHUNK, COLS), BF16),
            pltpu.VMEM((CHUNK, COLS), BF16),
            pltpu.VMEM((COLS, DIM), BF16),
            pltpu.VMEM((DIM, COLS), BF16),
            pltpu.VMEM((COLS, DIM), BF16),
            pltpu.VMEM((8, COLS), F32),
            pltpu.VMEM((8, COLS), F32),
            pltpu.VMEM((DIM, COLS), F32),
            pltpu.VMEM((DIM, COLS), F32),
        ],
        compiler_params=pltpu.CompilerParams(vmem_limit_bytes=56 * 1024 * 1024),
        cost_estimate=pl.CostEstimate(flops=8_000_000_000, bytes_accessed=8_000_000, transcendentals=4_000_000),
    )(tp, q, do, own, *gathered, swapped)


def finish_kernel(own_ref, near_ref, far_ref, dk_ref, dv_ref):
    total = own_ref[...].astype(F32) + near_ref[...].astype(F32) + far_ref[...].astype(F32)
    turned = total.T.astype(BF16)
    dk_ref[...] = turned[0:DIM]
    dv_ref[...] = turned[DIM:]


def finish(own, near, far):
    vmem = pl.BlockSpec(memory_space=pltpu.VMEM)
    shape = jax.ShapeDtypeStruct((DIM, PIECE), BF16)
    return pl.pallas_call(
        finish_kernel, out_shape=(shape, shape), in_specs=[vmem] * 3, out_specs=(vmem, vmem)
    )(own, near, far)


def shift(x, by):
    size = lax.axis_size("ctx")
    pairs = [(i, i + by) for i in range(size) if 0 <= i + by < size]
    return lax.ppermute(x, "ctx", pairs)


def swap(x):
    return lax.ppermute(x, "ctx", [(i, i ^ 1) for i in range(lax.axis_size("ctx"))])


def turn(x, by):
    return lax.ppermute(x, "tp", [(i, (i + by) % 4) for i in range(4)])


def local(queries, key_rows, values, grad_out, doc_ids):
    tp = lax.axis_index("tp")
    odd = lax.rem(lax.axis_index("ctx"), 2) == 1
    q = queries.transpose(1, 2, 0)
    do = grad_out.transpose(1, 2, 0)
    docs = jnp.broadcast_to((doc_ids + 1).astype(BF16)[None], (16, ROWS))
    own = jnp.concatenate([key_rows.T, values.T, docs], axis=0)

    def quarter_of(off):
        start = lax.rem(tp + off, 4) * PIECE
        return lax.dynamic_slice(own, (0, start), (PACKED, PIECE))

    mine = quarter_of(0)
    near = shift(mine, 2)
    far = shift(mine, 4)
    pair = jnp.stack([far, near])
    gathered = [pair, turn(pair, 1), turn(pair, -1), turn(pair, 2)]
    payload = jnp.stack(
        [
            jnp.where(odd, piece, jnp.stack([piece[1], quarter_of(off)]))
            for piece, off in zip(gathered, OFFSETS)
        ]
    )
    swapped = swap(payload)
    attended, dq, dkv = attend(tp.astype(jnp.int32)[None], q, do, own, gathered, swapped)
    back = swap(jnp.stack([dkv[1], dkv[3]])).astype(F32)
    a2, a1, a0 = dkv[0].astype(F32), dkv[2].astype(F32), dkv[4].astype(F32)
    a2 = a2 + jnp.where(odd, back[0], 0.0)
    a1 = a1 + jnp.where(odd, back[1], back[0])
    a0 = a0 + jnp.where(odd, 0.0, back[1])
    slots = [jnp.stack([a2[r], a1[r], a0[r]]).astype(BF16) for r in range(4)]
    summed = slots[0].astype(F32)
    for r, by in ((1, -1), (2, 1), (3, 2)):
        summed = summed + turn(slots[r], by).astype(F32)
    summed = summed.astype(BF16)
    dk, dv = finish(summed[2], shift(summed[1], -2), shift(summed[0], -4))
    return attended.transpose(2, 0, 1), dq.transpose(2, 0, 1), dk.T, dv.T


def solution(mesh):
    placed = (P("ctx", "tp", None), P("ctx", None), P("ctx", None), P("ctx", "tp", None), P("ctx"))
    return jax.shard_map(
        local,
        mesh=mesh,
        in_specs=placed,
        out_specs=(
            P("ctx", "tp", None),
            P("ctx", "tp", None),
            P(("ctx", "tp"), None),
            P(("ctx", "tp"), None),
        ),
        check_vma=False,
    )
```

```python
import jax
import jax.numpy as jnp
from jax import lax
from jax.experimental import pallas as pl
from jax.experimental.pallas import tpu as pltpu
from jax.sharding import PartitionSpec as P

LOG2E = 1.4426950408889634
NEGATIVE = -1e30
ROWS = 512
HALF = 256
PIECE = 128
DIM = 192
WIDE = 256
DOC_ROW = 2 * DIM
PACKED = DOC_ROW + 16
TILES = 4
HEADS = 3
COLS = HEADS * ROWS
SCALE = DIM ** -0.5
OFFSETS = (0, 3, 1, 2)
F32 = jnp.float32
BF16 = jnp.bfloat16
VMEM = pl.BlockSpec(memory_space=pltpu.VMEM)
SMEM = pl.BlockSpec(memory_space=pltpu.SMEM)


def dot(a, b):
    return jnp.dot(a, b, preferred_element_type=F32)


def head_cols(head, start=0):
    return slice(head * ROWS + start, (head + 1) * ROWS)


def one_hot(docs, width):
    rows = lax.broadcasted_iota(jnp.int32, (64, width), 0).astype(F32)
    return rows == docs.astype(F32)


def key_features(piece):
    hot = one_hot(piece[DOC_ROW : DOC_ROW + 1, :], piece.shape[1])
    return jnp.concatenate([piece[0:DIM, :], hot.astype(F32).astype(BF16)], axis=0).T


def folded(x):
    return x.reshape(x.shape[0] // 8, 8, x.shape[1])


def spread(row):
    return jnp.broadcast_to(row, (8, row.shape[1]))


def relative_slot(quarter, tp):
    off = lax.rem(quarter - tp + 4, 4)
    return jnp.where(off == 0, 0, jnp.where(off == 3, 1, off + 1))


def own_kernel(q_ref, own_ref, qe, qn, w_ref, top_ref, total_ref, o_ref):
    docs = own_ref[DOC_ROW : DOC_ROW + 1, :]
    mask_rows = jnp.where(one_hot(docs, ROWS), 0.0, NEGATIVE).astype(BF16)
    kn = key_features(own_ref[...])
    causal = lax.broadcasted_iota(jnp.int32, (HALF, HALF), 0) <= lax.broadcasted_iota(
        jnp.int32, (HALF, HALF), 1
    )
    for head in range(HEADS):
        cols = head_cols(head)
        low = slice(head * ROWS, head * ROWS + HALF)
        high = head_cols(head, HALF)
        qe[0:DIM, cols] = q_ref[head]
        qe[DIM:, cols] = mask_rows
        qn[cols, :] = q_ref[head].T
        s_low = jnp.where(causal, dot(kn[0:HALF], qe[:, low]), NEGATIVE)
        s_high = dot(kn, qe[:, high])
        s_top = s_high[0:HALF]
        s_last = jnp.where(causal, s_high[HALF:], NEGATIVE)
        for span, parts in ((low, (s_low,)), (high, (s_top, s_last))):
            peak = jnp.max(folded(parts[0]), axis=0)
            for s in parts[1:]:
                peak = jnp.maximum(peak, jnp.max(folded(s), axis=0))
            peak = spread(jnp.max(peak, axis=0, keepdims=True) * (SCALE * LOG2E))
            top_ref[:, span] = peak
            total = jnp.zeros((8, HALF), F32)
            for part, s in enumerate(parts):
                e = jnp.exp2(folded(s) * (SCALE * LOG2E) - peak[None])
                total = total + jnp.sum(e, axis=0)
                w_ref[part * HALF : (part + 1) * HALF, span] = e.reshape(HALF, HALF).astype(BF16)
            total_ref[:, span] = total
        o_ref[:, low] = dot(own_ref[DIM : 2 * DIM, 0:HALF], w_ref[0:HALF, low])
        o_ref[:, high] = dot(own_ref[DIM : 2 * DIM, :], w_ref[:, high])


def own_forward(q, own):
    return pl.pallas_call(
        own_kernel,
        out_shape=(
            jax.ShapeDtypeStruct((WIDE, COLS), BF16),
            jax.ShapeDtypeStruct((COLS, DIM), BF16),
            jax.ShapeDtypeStruct((ROWS, COLS), BF16),
            jax.ShapeDtypeStruct((8, COLS), F32),
            jax.ShapeDtypeStruct((8, COLS), F32),
            jax.ShapeDtypeStruct((DIM, COLS), F32),
        ),
        in_specs=[VMEM] * 2,
        out_specs=(VMEM,) * 6,
        compiler_params=pltpu.CompilerParams(vmem_limit_bytes=8 * 1024 * 1024),
        cost_estimate=pl.CostEstimate(flops=800_000_000, bytes_accessed=8_000_000, transcendentals=600_000),
    )(q, own)


def earlier_kernel(
    tp_ref, do_ref, docs_ref, qe, qn, top0_ref, total0_ref, o0_ref,
    a2_refs, a1_refs, sw_ref,
    o_ref, dkv_ref, ds_ref, kt, stats_ref, first_ref,
    vt, kn, vn, scores, weights, dop, don, top, total, oacc,
):
    tp = tp_ref[0]
    to_log2 = SCALE * LOG2E

    def piece_of(tile, slot):
        if tile % 2 == 0:
            return (a2_refs, a1_refs)[tile // 2][slot]
        return sw_ref.at[slot, tile // 2]

    first_doc = docs_ref[0:1, 0:1].astype(F32)
    matches = jnp.zeros((1, PIECE), F32)
    for tile in range(TILES):
        for slot in range(4):
            docs = piece_of(tile, slot)[DOC_ROW : DOC_ROW + 1, :].astype(F32)
            matches = matches + jnp.where(docs == first_doc, 1.0, 0.0)
    reach = jnp.sum(matches).astype(jnp.int32)
    first = (TILES * ROWS - reach) // ROWS
    first_ref[0] = first

    for tile in range(TILES):
        @pl.when(tile >= first)
        def _():
            for slot in range(4):
                start = lax.rem(tp + OFFSETS[slot], 4) * PIECE
                span = pl.ds(pl.multiple_of(start, PIECE), PIECE)
                piece = piece_of(tile, slot)[...]
                kt[tile, :, span] = piece[0:DIM, :]
                vt[tile, :, span] = piece[DIM : 2 * DIM, :]
                kn[tile, span, :] = key_features(piece)
                vn[tile, span, :] = piece[DIM : 2 * DIM, :].T

    top[...] = top0_ref[...] * (1.0 / to_log2)

    @pl.loop(first, TILES)
    def _(tile):
        for head in range(HEADS):
            cols = head_cols(head)
            s = dot(kn[tile], qe[:, cols])
            scores[tile, :, cols] = s
            top[:, cols] = jnp.maximum(top[:, cols], jnp.max(folded(s), axis=0))

    top[...] = spread(jnp.max(top[...], axis=0, keepdims=True) * to_log2)
    shrink = jnp.exp2(top0_ref[...] - top[...])
    total[...] = total0_ref[...] * shrink
    for head in range(HEADS):
        cols = head_cols(head)
        oacc[:, cols] = o0_ref[:, cols] * shrink[0:1, cols]

    @pl.loop(first, TILES)
    def _(tile):
        for head in range(HEADS):
            cols = head_cols(head)
            e = jnp.exp2(folded(scores[tile, :, cols]) * to_log2 - top[:, cols][None])
            total[:, cols] += jnp.sum(e, axis=0)
            w = e.reshape(ROWS, ROWS).astype(BF16)
            weights[tile, :, cols] = w
            oacc[:, cols] += dot(vt[tile], w)

    for head in range(HEADS):
        cols = head_cols(head)
        inverse = 1.0 / jnp.sum(total[:, cols], axis=0, keepdims=True)
        attended = (oacc[:, cols] * inverse).astype(BF16)
        o_ref[head] = attended
        grads = do_ref[head].astype(F32)
        delta = jnp.sum(grads * attended.astype(F32), axis=0, keepdims=True)
        ratio = inverse * SCALE
        top[:, cols] = spread(delta * ratio)
        stats_ref[0:8, cols] = spread(ratio * shrink[0:1, cols])
        stats_ref[8:16, cols] = spread(delta * ratio * shrink[0:1, cols])
        scaled = (grads * ratio).astype(BF16)
        dop[:, cols] = scaled
        don[cols, :] = scaled.T

    @pl.loop(first, TILES)
    def _(tile):
        for head in range(HEADS):
            cols = head_cols(head)
            dp = folded(dot(vn[tile], dop[:, cols]))
            w = folded(weights[tile, :, cols].astype(F32))
            ds_ref[tile, :, cols] = (w * (dp - top[:, cols][None])).reshape(ROWS, ROWS).astype(BF16)
        dk = dot(ds_ref[tile], qn[...])
        dv = dot(weights[tile], don[...])
        both = jnp.concatenate([dk, dv * (1.0 / SCALE)], axis=1).astype(BF16)
        for quarter in range(4):
            dkv_ref[tile, relative_slot(quarter, tp)] = both[quarter * PIECE : (quarter + 1) * PIECE]

    @pl.loop(0, first)
    def _(tile):
        dkv_ref[tile] = jnp.zeros((4, PIECE, 2 * DIM), BF16)


def earlier(tp, do, docs, own_parts, far, near, swapped):
    qe, qn, _, top, total, o = own_parts
    def kernel(*refs):
        earlier_kernel(*refs[:8], refs[8:12], refs[12:16], *refs[16:])
    return pl.pallas_call(
        kernel,
        out_shape=(
            jax.ShapeDtypeStruct((HEADS, DIM, ROWS), BF16),
            jax.ShapeDtypeStruct((TILES, 4, PIECE, 2 * DIM), BF16),
            jax.ShapeDtypeStruct((TILES, ROWS, COLS), BF16),
            jax.ShapeDtypeStruct((TILES, DIM, ROWS), BF16),
            jax.ShapeDtypeStruct((16, COLS), F32),
            jax.ShapeDtypeStruct((1,), jnp.int32),
        ),
        in_specs=[SMEM] + [VMEM] * 16,
        out_specs=(VMEM,) * 5 + (SMEM,),
        scratch_shapes=[
            pltpu.VMEM((TILES, DIM, ROWS), BF16),
            pltpu.VMEM((TILES, ROWS, WIDE), BF16),
            pltpu.VMEM((TILES, ROWS, DIM), BF16),
            pltpu.VMEM((TILES, ROWS, COLS), F32),
            pltpu.VMEM((TILES, ROWS, COLS), BF16),
            pltpu.VMEM((DIM, COLS), BF16),
            pltpu.VMEM((COLS, DIM), BF16),
            pltpu.VMEM((8, COLS), F32),
            pltpu.VMEM((8, COLS), F32),
            pltpu.VMEM((DIM, COLS), F32),
        ],
        compiler_params=pltpu.CompilerParams(vmem_limit_bytes=30 * 1024 * 1024),
        cost_estimate=pl.CostEstimate(flops=8_000_000_000, bytes_accessed=8_000_000, transcendentals=4_000_000),
    )(tp, do, docs, qe, qn, top, total, o, *far, *near, swapped)


def own_back_kernel(
    tp_ref, first_ref, do_ref, own_ref, qn, w_ref, stats_ref, ds_ref, kt,
    dq_ref, dkv_ref, ds_own, don, dqacc,
):
    tp = tp_ref[0]
    vn = own_ref[DIM : 2 * DIM, :].T
    for head in range(HEADS):
        cols = head_cols(head)
        low = slice(head * ROWS, head * ROWS + HALF)
        high = head_cols(head, HALF)
        scaled = (do_ref[head].astype(F32) * stats_ref[0:1, cols]).astype(BF16)
        don[cols, :] = scaled.T
        dp_low = dot(vn[0:HALF], scaled[:, 0:HALF])
        dp_high = dot(vn, scaled[:, HALF:])
        ds_own[0:HALF, low] = (
            w_ref[0:HALF, low].astype(F32) * (dp_low - stats_ref[8:9, low])
        ).astype(BF16)
        ds_own[:, high] = (w_ref[:, high].astype(F32) * (dp_high - stats_ref[8:9, high])).astype(BF16)
        dqacc[:, low] = dot(own_ref[0:DIM, 0:HALF], ds_own[0:HALF, low])
        dqacc[:, high] = dot(own_ref[0:DIM, :], ds_own[:, high])
    for part in range(2):
        span = slice(part * HALF, (part + 1) * HALF)
        dk = jnp.zeros((HALF, DIM), F32)
        dv = jnp.zeros((HALF, DIM), F32)
        for head in range(HEADS):
            cols = head_cols(head, part * HALF)
            dk = dk + dot(ds_own[span, cols], qn[cols, :])
            dv = dv + dot(w_ref[span, cols], don[cols, :])
        both = jnp.concatenate([dk, dv * (1.0 / SCALE)], axis=1).astype(BF16)
        for half in range(2):
            slot = relative_slot(part * 2 + half, tp)
            dkv_ref[slot] = both[half * PIECE : (half + 1) * PIECE]

    @pl.loop(first_ref[0], TILES)
    def _(tile):
        for head in range(HEADS):
            cols = head_cols(head)
            dqacc[:, cols] += dot(kt[tile], ds_ref[tile, :, cols])

    for head in range(HEADS):
        dq_ref[head] = dqacc[:, head_cols(head)].astype(BF16)


def own_back(tp, first, do, own, own_parts, stats, ds, kt):
    return pl.pallas_call(
        own_back_kernel,
        out_shape=(
            jax.ShapeDtypeStruct((HEADS, DIM, ROWS), BF16),
            jax.ShapeDtypeStruct((4, PIECE, 2 * DIM), BF16),
        ),
        in_specs=[SMEM, SMEM] + [VMEM] * 7,
        out_specs=(VMEM,) * 2,
        scratch_shapes=[
            pltpu.VMEM((ROWS, COLS), BF16),
            pltpu.VMEM((COLS, DIM), BF16),
            pltpu.VMEM((DIM, COLS), F32),
        ],
        compiler_params=pltpu.CompilerParams(vmem_limit_bytes=8 * 1024 * 1024),
        cost_estimate=pl.CostEstimate(flops=2_000_000_000, bytes_accessed=8_000_000, transcendentals=0),
    )(tp, first, do, own, own_parts[1], own_parts[2], stats, ds, kt)


def finish_kernel(*refs):
    total = refs[0][...].astype(F32)
    for ref in refs[1:-2]:
        total = total + ref[...].astype(F32)
    turned = total.T.astype(BF16)
    refs[-2][...] = turned[0:DIM]
    refs[-1][...] = turned[DIM:]


def finish(parts):
    shape = jax.ShapeDtypeStruct((DIM, PIECE), BF16)
    return pl.pallas_call(
        finish_kernel, out_shape=(shape, shape), in_specs=[VMEM] * len(parts), out_specs=(VMEM, VMEM)
    )(*parts)


def shift(x, by):
    size = lax.axis_size("ctx")
    pairs = [(i, i + by) for i in range(size) if 0 <= i + by < size]
    return lax.ppermute(x, "ctx", pairs)


def swap(x):
    return lax.ppermute(x, "ctx", [(i, i ^ 1) for i in range(lax.axis_size("ctx"))])


def turn(x, by):
    return lax.ppermute(x, "tp", [(i, (i + by) % 4) for i in range(4)])


def local(queries, key_rows, values, grad_out, doc_ids):
    tp = lax.axis_index("tp")
    tp_scalar = tp.astype(jnp.int32)[None]
    odd = lax.rem(lax.axis_index("ctx"), 2) == 1
    q = queries.transpose(1, 2, 0)
    do = grad_out.transpose(1, 2, 0)
    docs = jnp.broadcast_to((doc_ids + 1).astype(BF16)[None], (16, ROWS))
    own = jnp.concatenate([key_rows.T, values.T, docs], axis=0)

    def quarter_of(x, off):
        start = lax.rem(tp + off, 4) * PIECE
        return lax.dynamic_slice(x, (0, start), (PACKED, PIECE))

    far = shift(quarter_of(own, 0), 4)
    near_whole = shift(own, 2)
    own_parts = own_forward(q, own)
    far, own_parts = lax.optimization_barrier((far, own_parts))
    fars = [far, turn(far, 1), turn(far, -1), turn(far, 2)]
    nears = [quarter_of(near_whole, off) for off in OFFSETS]
    owns = [quarter_of(own, off) for off in OFFSETS]
    payload = jnp.stack(
        [jnp.stack([jnp.where(odd, f, n), jnp.where(odd, n, o)]) for f, n, o in zip(fars, nears, owns)]
    )
    swapped = swap(payload)
    attended, dkv, ds, kt, stats, first = earlier(tp_scalar, do, docs, own_parts, fars, nears, swapped)
    back = swap(jnp.stack([dkv[1], dkv[3]]))
    a2 = [dkv[0, r].astype(F32) + jnp.where(odd, back[0, r].astype(F32), 0.0) for r in range(4)]
    a1 = dkv[2].astype(F32) + jnp.where(odd, back[1], back[0]).astype(F32)
    a1_here = shift(a1.astype(BF16), -2)
    a2_sum = a2[0]
    for r, by in ((1, -1), (2, 1), (3, 2)):
        a2_sum = a2_sum + turn(a2[r].astype(BF16), by).astype(F32)
    a2_here = shift(a2_sum.astype(BF16), -4)
    dq, dkv_own = own_back(tp_scalar, first, do, own, own_parts, stats, ds, kt)
    a0 = [
        dkv_own[r].astype(F32) + a1_here[r].astype(F32) + jnp.where(odd, 0.0, back[1, r].astype(F32))
        for r in range(4)
    ]
    parts = [a0[0], a2_here]
    for r, by in ((1, -1), (2, 1), (3, 2)):
        parts.append(turn(a0[r].astype(BF16), by))
    dk, dv = finish(parts)
    return attended.transpose(2, 0, 1), dq.transpose(2, 0, 1), dk.T, dv.T


def solution(mesh):
    placed = (P("ctx", "tp", None), P("ctx", None), P("ctx", None), P("ctx", "tp", None), P("ctx"))
    return jax.shard_map(
        local,
        mesh=mesh,
        in_specs=placed,
        out_specs=(
            P("ctx", "tp", None),
            P("ctx", "tp", None),
            P(("ctx", "tp"), None),
            P(("ctx", "tp"), None),
        ),
        check_vma=False,
    )
```

```python
import jax
import jax.numpy as jnp
from jax import lax
from jax.experimental import pallas as pl
from jax.experimental.pallas import tpu as pltpu
from jax.sharding import PartitionSpec as P

LOG2E = 1.4426950408889634
NEGATIVE = -1e30
ROWS = 512
HALF = 256
PIECE = 128
DIM = 192
WIDE = 256
DOC_ROW = 2 * DIM
PACKED = DOC_ROW + 16
HEADS = 3
COLS = HEADS * ROWS
SCALE = DIM ** -0.5
TO_LOG2 = SCALE * LOG2E
OFFSETS = (0, 3, 1, 2)
RETURNS = ((1, -1), (2, 1), (3, 2))
F32 = jnp.float32
BF16 = jnp.bfloat16
VMEM = pl.BlockSpec(memory_space=pltpu.VMEM)
SMEM = pl.BlockSpec(memory_space=pltpu.SMEM)


def dot(a, b):
    return jnp.dot(a, b, preferred_element_type=F32)


def head_cols(head, start=0):
    return slice(head * ROWS + start, (head + 1) * ROWS)


def one_hot(docs, width):
    rows = lax.broadcasted_iota(jnp.int32, (64, width), 0).astype(F32)
    return rows == docs.astype(F32)


def key_features(piece):
    hot = one_hot(piece[DOC_ROW : DOC_ROW + 1, :], piece.shape[1])
    return jnp.concatenate([piece[0:DIM, :], hot.astype(F32).astype(BF16)], axis=0).T


def folded(x):
    return x.reshape(x.shape[0] // 8, 8, x.shape[1])


def spread(row):
    return jnp.broadcast_to(row, (8, row.shape[1]))


def call(kernel, outs, operands, smem, scratch, limit, flops):
    return pl.pallas_call(
        kernel,
        out_shape=tuple(jax.ShapeDtypeStruct(shape, dtype) for shape, dtype in outs),
        in_specs=[SMEM if i in smem else VMEM for i in range(len(operands))],
        out_specs=tuple(SMEM if dtype == jnp.int32 else VMEM for _, dtype in outs),
        scratch_shapes=[pltpu.VMEM(shape, dtype) for shape, dtype in scratch],
        compiler_params=pltpu.CompilerParams(vmem_limit_bytes=limit * 1024 * 1024),
        cost_estimate=pl.CostEstimate(flops=flops, bytes_accessed=8_000_000, transcendentals=1_000_000),
    )(*operands)


def own_kernel(q_ref, own_ref, qe, qn, w_ref, top_ref, total_ref, o_ref):
    docs = own_ref[DOC_ROW : DOC_ROW + 1, :]
    mask_rows = jnp.where(one_hot(docs, ROWS), 0.0, NEGATIVE).astype(BF16)
    kn = key_features(own_ref[...])
    causal = lax.broadcasted_iota(jnp.int32, (HALF, HALF), 0) <= lax.broadcasted_iota(
        jnp.int32, (HALF, HALF), 1
    )
    for head in range(HEADS):
        cols = head_cols(head)
        low = slice(head * ROWS, head * ROWS + HALF)
        high = head_cols(head, HALF)
        qe[0:DIM, cols] = q_ref[head]
        qe[DIM:, cols] = mask_rows
        qn[cols, :] = q_ref[head].T
        s_low = jnp.where(causal, dot(kn[0:HALF], qe[:, low]), NEGATIVE)
        s_high = dot(kn, qe[:, high])
        s_top = s_high[0:HALF]
        s_last = jnp.where(causal, s_high[HALF:], NEGATIVE)
        for span, parts in ((low, (s_low,)), (high, (s_top, s_last))):
            peak = jnp.max(folded(parts[0]), axis=0)
            for s in parts[1:]:
                peak = jnp.maximum(peak, jnp.max(folded(s), axis=0))
            peak = spread(jnp.max(peak, axis=0, keepdims=True) * TO_LOG2)
            top_ref[:, span] = peak
            total = jnp.zeros((8, HALF), F32)
            for part, s in enumerate(parts):
                e = jnp.exp2(folded(s) * TO_LOG2 - peak[None])
                total = total + jnp.sum(e, axis=0)
                w_ref[part * HALF : (part + 1) * HALF, span] = e.reshape(HALF, HALF).astype(BF16)
            total_ref[:, span] = total
        o_ref[:, low] = dot(own_ref[DIM : 2 * DIM, 0:HALF], w_ref[0:HALF, low])
        o_ref[:, high] = dot(own_ref[DIM : 2 * DIM, :], w_ref[:, high])


def own_forward(q, own):
    outs = [
        ((WIDE, COLS), BF16), ((COLS, DIM), BF16), ((ROWS, COLS), BF16),
        ((8, COLS), F32), ((8, COLS), F32), ((DIM, COLS), F32),
    ]
    return call(own_kernel, outs, [q, own], (), [], 8, 800_000_000)


def needed_flag(rows, first_doc):
    matches = jnp.zeros((1, PIECE), F32)
    for row in rows:
        for start in range(0, row.shape[1], PIECE):
            docs = row[:, start : start + PIECE].astype(F32)
            matches = matches + jnp.where(docs == first_doc, 1.0, 0.0)
    return (jnp.max(matches) > 0.0).astype(jnp.int32)


def flag_row(flag):
    return jnp.broadcast_to(flag.astype(F32), (1, COLS))


def read_flag(ref, row):
    return (jnp.max(ref[row : row + 1, 0:PIECE]) > 0.0).astype(jnp.int32)


def score_pass(flags, tiles, kn, vts, qe, scores, w_ref, top0, total0, o0, top, total, o):
    top[...] = top0[...]

    for tile in range(tiles):
        @pl.when(flags[tile] > 0)
        def _():
            for head in range(HEADS):
                cols = head_cols(head)
                s = dot(kn[tile], qe[:, cols]) * TO_LOG2
                scores[tile, :, cols] = s
                top[:, cols] = jnp.maximum(top[:, cols], jnp.max(folded(s), axis=0))

    top[...] = spread(jnp.max(top[...], axis=0, keepdims=True))
    shrink = jnp.exp2(top0[...] - top[...])
    total[...] = total0[...] * shrink
    for head in range(HEADS):
        cols = head_cols(head)
        o[:, cols] = o0[:, cols] * shrink[0:1, cols]

    for tile in range(tiles):
        @pl.when(flags[tile] > 0)
        def _():
            for head in range(HEADS):
                cols = head_cols(head)
                e = jnp.exp2(folded(scores[tile, :, cols]) - top[:, cols][None])
                total[:, cols] += jnp.sum(e, axis=0)
                w = e.reshape(ROWS, ROWS).astype(BF16)
                w_ref[tile, :, cols] = w
                o[:, cols] += dot(vts[tile](), w)


def near_kernel(
    near_ref, near_sib_ref, own_sib_ref, own_ref, qe, top0, total0, o0,
    w_ref, vn, top, total, o, flag_ref,
    kn, scores,
):
    refs = (near_ref, near_sib_ref, own_sib_ref)
    first_doc = own_ref[DOC_ROW : DOC_ROW + 1, 0:1].astype(F32)
    flags = [needed_flag([ref[DOC_ROW : DOC_ROW + 1, :]], first_doc) for ref in refs]
    for tile in range(3):
        flag_ref[tile : tile + 1, :] = flag_row(flags[tile])
    for tile, ref in enumerate(refs):
        @pl.when(flags[tile] > 0)
        def _():
            kn[tile] = key_features(ref[...])
            vn[tile] = ref[DIM : 2 * DIM, :].T
    vts = [lambda ref=ref: ref[DIM : 2 * DIM, :] for ref in refs]
    score_pass(flags, 3, kn, vts, qe, scores, w_ref, top0, total0, o0, top, total, o)


def near_forward(near, near_sib, own_sib, own, own_parts):
    qe, _, _, top, total, o = own_parts
    outs = [
        ((3, ROWS, COLS), BF16), ((3, ROWS, DIM), BF16),
        ((8, COLS), F32), ((8, COLS), F32), ((DIM, COLS), F32), ((8, COLS), F32),
    ]
    scratch = [((3, ROWS, WIDE), BF16), ((3, ROWS, COLS), F32)]
    operands = [near, near_sib, own_sib, own, qe, top, total, o]
    return call(near_kernel, outs, operands, (), scratch, 14, 3_000_000_000)


def grad_tile(tile, flag, w, vn, dop, don, delta, qn, ds_ref, out):
    @pl.when(flag > 0)
    def _():
        for head in range(HEADS):
            cols = head_cols(head)
            dp = folded(dot(vn[tile], dop[:, cols]))
            wide = folded(w[tile, :, cols].astype(F32))
            ds = (wide * (dp - delta[:, cols][None])).reshape(ROWS, ROWS)
            ds_ref[tile, :, cols] = ds.astype(BF16)
        dk = dot(ds_ref[tile], qn[...])
        dv = dot(w[tile], don[...])
        out[...] = jnp.concatenate([dk, dv * (1.0 / SCALE)], axis=1).astype(BF16)

    @pl.when(flag == 0)
    def _():
        out[...] = jnp.zeros((ROWS, 2 * DIM), BF16)


def scaled_grads(do_ref, ratio, dop, don):
    for head in range(HEADS):
        cols = head_cols(head)
        scaled = (do_ref[head].astype(F32) * ratio[0:1, cols]).astype(BF16)
        dop[:, cols] = scaled
        don[cols, :] = scaled.T


def middle_kernel(
    near_flag_ref, do_ref, own_ref, qe, qn, top_own, near_w, near_vn, top_near, total_near, o_near,
    f0_ref, f1_ref, f2_ref, f3_ref, far_sib_ref,
    o_ref, dnear_ref, dfar_ref, dsib_ref, near_ds, far_ds, far_kt, stats,
    kn, vt, far_vn, far_w, scores, top, total, o, dop, don,
):
    fars = (f0_ref, f1_ref, f2_ref, f3_ref)
    sibs = tuple(far_sib_ref.at[r] for r in range(4))
    doc_row = slice(DOC_ROW, DOC_ROW + 1)
    first_doc = own_ref[doc_row, 0:1].astype(F32)
    near_flags = [read_flag(near_flag_ref, tile) for tile in range(3)]
    far_flags = [needed_flag([ref[doc_row, :] for ref in refs], first_doc) for refs in (fars, sibs)]
    for i, flag in enumerate(near_flags + far_flags):
        stats[48 + i : 49 + i, :] = flag_row(flag)
    for tile, refs in enumerate((fars, sibs)):
        @pl.when(far_flags[tile] > 0)
        def _():
            for r, ref in enumerate(refs):
                span = slice(r * PIECE, (r + 1) * PIECE)
                piece = ref[...]
                kn[tile, span, :] = key_features(piece)
                far_vn[tile, span, :] = piece[DIM : 2 * DIM, :].T
                far_kt[tile, :, span] = piece[0:DIM, :]
                vt[tile, :, span] = piece[DIM : 2 * DIM, :]
    vts = [lambda tile=tile: vt[tile] for tile in range(2)]
    score_pass(far_flags, 2, kn, vts, qe, scores, far_w, top_near, total_near, o_near, top, total, o)

    near_shrink = jnp.exp2(top_near[...] - top[...])
    own_shrink = jnp.exp2(top_own[...] - top[...])
    for head in range(HEADS):
        cols = head_cols(head)
        inverse = 1.0 / jnp.sum(total[:, cols], axis=0, keepdims=True)
        attended = (o[:, cols] * inverse).astype(BF16)
        o_ref[head] = attended
        delta = jnp.sum(do_ref[head].astype(F32) * attended.astype(F32), axis=0, keepdims=True)
        ratio = spread(inverse * SCALE)
        for i, shrink in enumerate((None, near_shrink, own_shrink)):
            part = ratio if shrink is None else ratio * shrink[:, cols]
            stats[i * 16 : i * 16 + 8, cols] = part
            stats[i * 16 + 8 : i * 16 + 16, cols] = part * delta

    scaled_grads(do_ref, stats.at[16:24], dop, don)
    delta = stats.at[24:32]
    grad_tile(0, near_flags[0], near_w, near_vn, dop, don, delta, qn, near_ds, dnear_ref)
    grad_tile(1, near_flags[1], near_w, near_vn, dop, don, delta, qn, near_ds, dsib_ref.at[0])
    grad_tile(2, near_flags[2], near_w, near_vn, dop, don, delta, qn, near_ds, dsib_ref.at[1])
    scaled_grads(do_ref, stats.at[0:8], dop, don)
    delta = stats.at[8:16]
    grad_tile(0, far_flags[0], far_w, far_vn, dop, don, delta, qn, far_ds, dfar_ref)

    @pl.when(far_flags[1] > 0)
    def _():
        grad_tile(1, far_flags[1], far_w, far_vn, dop, don, delta, qn, far_ds, dsib_ref.at[1])


def middle(do, own, own_parts, near_parts, fars, far_sib):
    qe, qn, _, top_own, _, _ = own_parts
    near_w, near_vn, top, total, o, flags = near_parts
    outs = [
        ((HEADS, DIM, ROWS), BF16), ((ROWS, 2 * DIM), BF16), ((ROWS, 2 * DIM), BF16), ((2, ROWS, 2 * DIM), BF16),
        ((3, ROWS, COLS), BF16), ((2, ROWS, COLS), BF16), ((2, DIM, ROWS), BF16), ((56, COLS), F32),
    ]
    scratch = [
        ((2, ROWS, WIDE), BF16), ((2, DIM, ROWS), BF16), ((2, ROWS, DIM), BF16), ((2, ROWS, COLS), BF16),
        ((2, ROWS, COLS), F32),
        ((8, COLS), F32), ((8, COLS), F32), ((DIM, COLS), F32), ((DIM, COLS), BF16), ((COLS, DIM), BF16),
    ]
    operands = [flags, do, own, qe, qn, top_own, near_w, near_vn, top, total, o, *fars, far_sib]
    return call(middle_kernel, outs, operands, (), scratch, 18, 6_000_000_000)


def own_back_kernel(
    do_ref, own_ref, qn, w_ref, stats,
    near_ref, near_sib_ref, own_sib_ref, far_kt, near_ds, far_ds,
    dq_ref, dkv_ref,
    ds_own, don, dqacc,
):
    vn = own_ref[DIM : 2 * DIM, :].T
    for head in range(HEADS):
        cols = head_cols(head)
        low = slice(head * ROWS, head * ROWS + HALF)
        high = head_cols(head, HALF)
        scaled = (do_ref[head].astype(F32) * stats[32:33, cols]).astype(BF16)
        don[cols, :] = scaled.T
        dp_low = dot(vn[0:HALF], scaled[:, 0:HALF])
        dp_high = dot(vn, scaled[:, HALF:])
        ds_own[0:HALF, low] = (w_ref[0:HALF, low].astype(F32) * (dp_low - stats[40:41, low])).astype(BF16)
        ds_own[:, high] = (w_ref[:, high].astype(F32) * (dp_high - stats[40:41, high])).astype(BF16)
        dqacc[:, low] = dot(own_ref[0:DIM, 0:HALF], ds_own[0:HALF, low])
        dqacc[:, high] = dot(own_ref[0:DIM, :], ds_own[:, high])
    for part in range(2):
        span = slice(part * HALF, (part + 1) * HALF)
        dk = jnp.zeros((HALF, DIM), F32)
        dv = jnp.zeros((HALF, DIM), F32)
        for head in range(HEADS):
            cols = head_cols(head, part * HALF)
            dk = dk + dot(ds_own[span, cols], qn[cols, :])
            dv = dv + dot(w_ref[span, cols], don[cols, :])
        dkv_ref[span, :] = jnp.concatenate([dk, dv * (1.0 / SCALE)], axis=1).astype(BF16)

    tiles = (
        (near_ref.at[0:DIM], near_ds.at[0]),
        (near_sib_ref.at[0:DIM], near_ds.at[1]),
        (own_sib_ref.at[0:DIM], near_ds.at[2]),
        (far_kt.at[0], far_ds.at[0]),
        (far_kt.at[1], far_ds.at[1]),
    )
    for i, (kt, ds) in enumerate(tiles):
        @pl.when(read_flag(stats, 48 + i) > 0)
        def _():
            for head in range(HEADS):
                cols = head_cols(head)
                dqacc[:, cols] += dot(kt[...], ds[:, cols])

    for head in range(HEADS):
        dq_ref[head] = dqacc[:, head_cols(head)].astype(BF16)


def own_back(do, own, near, near_sib, own_sib, own_parts, middle_parts):
    outs = [((HEADS, DIM, ROWS), BF16), ((ROWS, 2 * DIM), BF16)]
    scratch = [((ROWS, COLS), BF16), ((COLS, DIM), BF16), ((DIM, COLS), F32)]
    near_ds, far_ds, far_kt, stats = middle_parts
    operands = [do, own, own_parts[1], own_parts[2], stats, near, near_sib, own_sib, far_kt, near_ds, far_ds]
    return call(own_back_kernel, outs, operands, (), scratch, 8, 2_000_000_000)


def finish_kernel(*refs):
    total = refs[0][...].astype(F32)
    for ref in refs[1:-2]:
        total = total + ref[...].astype(F32)
    turned = total.T.astype(BF16)
    refs[-2][...] = turned[0:DIM]
    refs[-1][...] = turned[DIM:]


def finish(parts):
    shape = jax.ShapeDtypeStruct((DIM, PIECE), BF16)
    return pl.pallas_call(
        finish_kernel, out_shape=(shape, shape), in_specs=[VMEM] * len(parts), out_specs=(VMEM, VMEM),
        compiler_params=pltpu.CompilerParams(vmem_limit_bytes=4 * 1024 * 1024),
    )(*parts)


def shift(x, by):
    size = lax.axis_size("ctx")
    pairs = [(i, i + by) for i in range(size) if 0 <= i + by < size]
    return lax.ppermute(x, "ctx", pairs)


def swap(x):
    return lax.ppermute(x, "ctx", [(i, i ^ 1) for i in range(lax.axis_size("ctx"))])


def to_sibling(x, source):
    pairs = [(i, i ^ 1) for i in range(lax.axis_size("ctx")) if i % 2 == source]
    return lax.ppermute(x, "ctx", pairs)


def turn(x, by):
    return lax.ppermute(x, "tp", [(i, (i + by) % 4) for i in range(4)])


def local(queries, key_rows, values, grad_out, doc_ids):
    tp = lax.axis_index("tp")
    odd = lax.rem(lax.axis_index("ctx"), 2) == 1
    q = queries.transpose(1, 2, 0)
    do = grad_out.transpose(1, 2, 0)
    docs = jnp.broadcast_to((doc_ids + 1).astype(BF16)[None], (16, ROWS))
    own = jnp.concatenate([key_rows.T, values.T, docs], axis=0)
    starts = [lax.rem(tp + off, 4) * PIECE for off in OFFSETS]
    own, starts, odd = lax.optimization_barrier((own, starts, odd))
    zero = jnp.zeros((), starts[0].dtype)
    mine = lax.dynamic_slice(own, (zero, starts[0]), (PACKED, PIECE), allow_negative_indices=False)
    far = shift(mine, 4)
    near = shift(own, 2)
    own_sib = to_sibling(own, 0)
    own_parts = own_forward(q, own)
    far, near, own_sib, own_parts = lax.optimization_barrier((far, near, own_sib, own_parts))
    fars = [far, turn(far, 1), turn(far, -1), turn(far, 2)]
    near_sib = swap(near)
    near_parts = near_forward(near, near_sib, own_sib, own, own_parts)
    fars, near_parts = lax.optimization_barrier((fars, near_parts))
    far_sib = to_sibling(jnp.stack(fars), 1)
    middle_parts = middle(do, own, own_parts, near_parts, fars, far_sib)
    attended, dnear, dfar, dsib = middle_parts[:4]
    middle_parts = middle_parts[4:]
    back = swap(dsib)
    a1 = (dnear.astype(F32) + back[0].astype(F32)).astype(BF16)
    a2 = (dfar.astype(F32) + jnp.where(odd, back[1].astype(F32), 0.0)).astype(BF16)
    a2 = [a2[r * PIECE : (r + 1) * PIECE] for r in range(4)]
    a1, a2, middle_parts = lax.optimization_barrier((a1, a2, middle_parts))
    a1_here = shift(a1, -2)
    moved = [turn(a2[r], by) for r, by in RETURNS]
    dq, down = own_back(do, own, near, near_sib, own_sib, own_parts, middle_parts)
    moved, down = lax.optimization_barrier((moved, down))
    a2_sum = a2[0].astype(F32)
    for piece in moved:
        a2_sum = a2_sum + piece.astype(F32)
    a2_here = shift(a2_sum.astype(BF16), -4)
    a0 = down.astype(F32) + a1_here.astype(F32) + jnp.where(odd, 0.0, back[1].astype(F32))
    a0 = [
        lax.dynamic_slice(a0, (start, zero), (PIECE, 2 * DIM), allow_negative_indices=False).astype(BF16)
        for start in starts
    ]
    parts = [a0[0], a2_here] + [turn(a0[r], by) for r, by in RETURNS]
    dk, dv = finish(parts)
    return attended.transpose(2, 0, 1), dq.transpose(2, 0, 1), dk.T, dv.T


def solution(mesh):
    placed = (P("ctx", "tp", None), P("ctx", None), P("ctx", None), P("ctx", "tp", None), P("ctx"))
    return jax.shard_map(
        local,
        mesh=mesh,
        in_specs=placed,
        out_specs=(
            P("ctx", "tp", None),
            P("ctx", "tp", None),
            P(("ctx", "tp"), None),
            P(("ctx", "tp"), None),
        ),
        check_vma=False,
    )
```

```python
import jax
import jax.numpy as jnp
from jax import lax
from jax.experimental import pallas as pl
from jax.experimental.pallas import tpu as pltpu
from jax.sharding import PartitionSpec as P

LOG2E = 1.4426950408889634
NEGATIVE = -1e30
ROWS = 512
HALF = 256
PIECE = 128
DIM = 192
WIDE = 256
DOC_ROW = 2 * DIM
PACKED = DOC_ROW + 16
HEADS = 3
COLS = HEADS * ROWS
SCALE = DIM ** -0.5
TO_LOG2 = SCALE * LOG2E
OFFSETS = (0, 3, 1, 2)
RETURNS = ((1, -1), (2, 1), (3, 2))
F32 = jnp.float32
BF16 = jnp.bfloat16
VMEM = pl.BlockSpec(memory_space=pltpu.VMEM)
SMEM = pl.BlockSpec(memory_space=pltpu.SMEM)


def dot(a, b):
    return jnp.dot(a, b, preferred_element_type=F32)


def head_cols(head, start=0):
    return slice(head * ROWS + start, (head + 1) * ROWS)


def one_hot(docs, width):
    rows = lax.broadcasted_iota(jnp.int32, (64, width), 0).astype(F32)
    return rows == docs.astype(F32)


def key_features(piece):
    hot = one_hot(piece[DOC_ROW : DOC_ROW + 1, :], piece.shape[1])
    return jnp.concatenate([piece[0:DIM, :], hot.astype(F32).astype(BF16)], axis=0).T


def folded(x):
    return x.reshape(x.shape[0] // 8, 8, x.shape[1])


def spread(row):
    return jnp.broadcast_to(row, (8, row.shape[1]))


def call(kernel, outs, operands, smem, scratch, limit, flops):
    return pl.pallas_call(
        kernel,
        out_shape=tuple(jax.ShapeDtypeStruct(shape, dtype) for shape, dtype in outs),
        in_specs=[SMEM if i in smem else VMEM for i in range(len(operands))],
        out_specs=tuple(SMEM if dtype == jnp.int32 else VMEM for _, dtype in outs),
        scratch_shapes=[pltpu.VMEM(shape, dtype) for shape, dtype in scratch],
        compiler_params=pltpu.CompilerParams(vmem_limit_bytes=limit * 1024 * 1024),
        cost_estimate=pl.CostEstimate(flops=flops, bytes_accessed=8_000_000, transcendentals=1_000_000),
    )(*operands)


def own_kernel(q_ref, own_ref, qe, qn, w_ref, top_ref, total_ref, o_ref):
    docs = own_ref[DOC_ROW : DOC_ROW + 1, :]
    mask_rows = jnp.where(one_hot(docs, ROWS), 0.0, NEGATIVE).astype(BF16)
    kn = key_features(own_ref[...])
    causal = lax.broadcasted_iota(jnp.int32, (HALF, HALF), 0) <= lax.broadcasted_iota(
        jnp.int32, (HALF, HALF), 1
    )
    for head in range(HEADS):
        cols = head_cols(head)
        low = slice(head * ROWS, head * ROWS + HALF)
        high = head_cols(head, HALF)
        qe[0:DIM, cols] = q_ref[head]
        qe[DIM:, cols] = mask_rows
        qn[cols, :] = q_ref[head].T
        s_low = jnp.where(causal, dot(kn[0:HALF], qe[:, low]), NEGATIVE)
        s_high = dot(kn, qe[:, high])
        s_top = s_high[0:HALF]
        s_last = jnp.where(causal, s_high[HALF:], NEGATIVE)
        for span, parts in ((low, (s_low,)), (high, (s_top, s_last))):
            peak = jnp.max(folded(parts[0]), axis=0)
            for s in parts[1:]:
                peak = jnp.maximum(peak, jnp.max(folded(s), axis=0))
            peak = spread(jnp.max(peak, axis=0, keepdims=True) * TO_LOG2)
            top_ref[:, span] = peak
            total = jnp.zeros((8, HALF), F32)
            for part, s in enumerate(parts):
                e = jnp.exp2(folded(s) * TO_LOG2 - peak[None])
                total = total + jnp.sum(e, axis=0)
                w_ref[part * HALF : (part + 1) * HALF, span] = e.reshape(HALF, HALF).astype(BF16)
            total_ref[:, span] = total
        o_ref[:, low] = dot(own_ref[DIM : 2 * DIM, 0:HALF], w_ref[0:HALF, low])
        o_ref[:, high] = dot(own_ref[DIM : 2 * DIM, :], w_ref[:, high])


def own_forward(q, own):
    outs = [
        ((WIDE, COLS), BF16), ((COLS, DIM), BF16), ((ROWS, COLS), BF16),
        ((8, COLS), F32), ((8, COLS), F32), ((DIM, COLS), F32),
    ]
    return call(own_kernel, outs, [q, own], (), [], 8, 800_000_000)


def needed_flag(rows, first_doc):
    matches = jnp.zeros((1, PIECE), F32)
    for row in rows:
        for start in range(0, row.shape[1], PIECE):
            docs = row[:, start : start + PIECE].astype(F32)
            matches = matches + jnp.where(docs == first_doc, 1.0, 0.0)
    return (jnp.max(matches) > 0.0).astype(jnp.int32)


def flag_row(flag):
    return jnp.broadcast_to(flag.astype(F32), (1, COLS))


def read_flag(ref, row):
    return (jnp.max(ref[row : row + 1, 0:PIECE]) > 0.0).astype(jnp.int32)


def score_pass(flags, tiles, kn, vts, qe, scores, w_ref, top0, total0, o0, top, total, o):
    top[...] = top0[...]

    for tile in range(tiles):
        @pl.when(flags[tile] > 0)
        def _():
            for head in range(HEADS):
                cols = head_cols(head)
                s = dot(kn[tile], qe[:, cols]) * TO_LOG2
                scores[tile, :, cols] = s
                top[:, cols] = jnp.maximum(top[:, cols], jnp.max(folded(s), axis=0))

    top[...] = spread(jnp.max(top[...], axis=0, keepdims=True))
    shrink = jnp.exp2(top0[...] - top[...])
    total[...] = total0[...] * shrink
    for head in range(HEADS):
        cols = head_cols(head)
        o[:, cols] = o0[:, cols] * shrink[0:1, cols]

    for tile in range(tiles):
        @pl.when(flags[tile] > 0)
        def _():
            for head in range(HEADS):
                cols = head_cols(head)
                e = jnp.exp2(folded(scores[tile, :, cols]) - top[:, cols][None])
                total[:, cols] += jnp.sum(e, axis=0)
                w = e.reshape(ROWS, ROWS).astype(BF16)
                w_ref[tile, :, cols] = w
                o[:, cols] += dot(vts[tile](), w)


def prepare(refs, own_ref, kn, vn):
    first_doc = own_ref[DOC_ROW : DOC_ROW + 1, 0:1].astype(F32)
    flags = [needed_flag([ref[DOC_ROW : DOC_ROW + 1, :]], first_doc) for ref in refs]
    for tile, ref in enumerate(refs):
        @pl.when(flags[tile] > 0)
        def _():
            kn[tile] = key_features(ref[...])
            vn[tile] = ref[DIM : 2 * DIM, :].T
    return flags


def early_kernel(
    near_ref, far_ref, own_ref, qe, top0, total0, o0,
    w_ref, vn, top, total, o, flag_ref,
    kn, scores,
):
    refs = (near_ref, far_ref)
    flags = prepare(refs, own_ref, kn, vn)
    for tile in range(2):
        flag_ref[tile : tile + 1, :] = flag_row(flags[tile])
    vts = [lambda ref=ref: ref[DIM : 2 * DIM, :] for ref in refs]
    score_pass(flags, 2, kn, vts, qe, scores, w_ref, top0, total0, o0, top, total, o)


def early_forward(near, far, own, own_parts):
    qe, _, _, top, total, o = own_parts
    outs = [
        ((2, ROWS, COLS), BF16), ((2, ROWS, DIM), BF16),
        ((8, COLS), F32), ((8, COLS), F32), ((DIM, COLS), F32), ((8, COLS), F32),
    ]
    scratch = [((2, ROWS, WIDE), BF16), ((2, ROWS, COLS), F32)]
    operands = [near, far, own, qe, top, total, o]
    return call(early_kernel, outs, operands, (), scratch, 12, 3_000_000_000)


def grad_tile(tile, flag, w, vn, dop, don, delta, qn, ds_ref, out):
    @pl.when(flag > 0)
    def _():
        for head in range(HEADS):
            cols = head_cols(head)
            dp = folded(dot(vn[tile], dop[:, cols]))
            wide = folded(w[tile, :, cols].astype(F32))
            ds = (wide * (dp - delta[:, cols][None])).reshape(ROWS, ROWS)
            ds_ref[tile, :, cols] = ds.astype(BF16)
        dk = dot(ds_ref[tile], qn[...])
        dv = dot(w[tile], don[...])
        out[...] = jnp.concatenate([dk, dv * (1.0 / SCALE)], axis=1).astype(BF16)

    @pl.when(flag == 0)
    def _():
        out[...] = jnp.zeros((ROWS, 2 * DIM), BF16)


def scaled_grads(do_ref, ratio, dop, don):
    for head in range(HEADS):
        cols = head_cols(head)
        scaled = (do_ref[head].astype(F32) * ratio[0:1, cols]).astype(BF16)
        dop[:, cols] = scaled
        don[cols, :] = scaled.T


def middle_kernel(
    early_flag_ref, do_ref, own_ref, qe, qn, top_own, early_w, early_vn, top_early, total_early, o_early,
    near_sib_ref, far_sib_ref, own_sib_ref,
    o_ref, dnear_ref, dnear_sib_ref, near_ds, near_sib_ds, late_w, late_vn, stats, dop_early, don_early, dop, don,
    kn, scores, top, total, o,
):
    refs = (near_sib_ref, far_sib_ref, own_sib_ref)
    late_flags = prepare(refs, own_ref, kn, late_vn)
    early_flags = [read_flag(early_flag_ref, tile) for tile in range(2)]
    for i, flag in enumerate(early_flags + late_flags):
        stats[48 + i : 49 + i, :] = flag_row(flag)
    vts = [lambda ref=ref: ref[DIM : 2 * DIM, :] for ref in refs]
    score_pass(late_flags, 3, kn, vts, qe, scores, late_w, top_early, total_early, o_early, top, total, o)

    early_shrink = jnp.exp2(top_early[...] - top[...])
    own_shrink = jnp.exp2(top_own[...] - top[...])
    for head in range(HEADS):
        cols = head_cols(head)
        inverse = 1.0 / jnp.sum(total[:, cols], axis=0, keepdims=True)
        attended = (o[:, cols] * inverse).astype(BF16)
        o_ref[head] = attended
        delta = jnp.sum(do_ref[head].astype(F32) * attended.astype(F32), axis=0, keepdims=True)
        ratio = spread(inverse * SCALE)
        for i, shrink in enumerate((None, early_shrink, own_shrink)):
            part = ratio if shrink is None else ratio * shrink[:, cols]
            stats[i * 16 : i * 16 + 8, cols] = part
            stats[i * 16 + 8 : i * 16 + 16, cols] = part * delta

    scaled_grads(do_ref, stats.at[16:24], dop_early, don_early)
    scaled_grads(do_ref, stats.at[0:8], dop, don)
    grad_tile(0, early_flags[0], early_w, early_vn, dop_early, don_early, stats.at[24:32], qn, near_ds, dnear_ref)
    grad_tile(0, late_flags[0], late_w, late_vn, dop, don, stats.at[8:16], qn, near_sib_ds, dnear_sib_ref)


def middle(do, own, own_parts, early_parts, near_sib, far_sib, own_sib):
    qe, qn, _, top_own, _, _ = own_parts
    early_w, early_vn, top, total, o, flags = early_parts
    outs = [
        ((HEADS, DIM, ROWS), BF16), ((ROWS, 2 * DIM), BF16), ((ROWS, 2 * DIM), BF16),
        ((1, ROWS, COLS), BF16), ((1, ROWS, COLS), BF16),
        ((3, ROWS, COLS), BF16), ((3, ROWS, DIM), BF16), ((56, COLS), F32),
        ((DIM, COLS), BF16), ((COLS, DIM), BF16), ((DIM, COLS), BF16), ((COLS, DIM), BF16),
    ]
    scratch = [
        ((3, ROWS, WIDE), BF16), ((3, ROWS, COLS), F32),
        ((8, COLS), F32), ((8, COLS), F32), ((DIM, COLS), F32),
    ]
    operands = [
        flags, do, own, qe, qn, top_own, early_w, early_vn, top, total, o, near_sib, far_sib, own_sib
    ]
    return call(middle_kernel, outs, operands, (), scratch, 18, 5_000_000_000)


def last_kernel(
    qn, early_w, early_vn, late_w, late_vn, stats, dop_early, don_early, dop, don,
    dfar_ref, dsib_ref, far_ds, sib_ds,
):
    early_delta = stats.at[24:32]
    delta = stats.at[8:16]
    grad_tile(
        0, read_flag(stats, 49), early_w.at[1:2], early_vn.at[1:2], dop_early, don_early, early_delta, qn, far_ds,
        dfar_ref,
    )
    own_sib_flag = read_flag(stats, 52)
    grad_tile(0, read_flag(stats, 51), late_w.at[1:2], late_vn.at[1:2], dop, don, delta, qn, sib_ds, dsib_ref)

    @pl.when(own_sib_flag > 0)
    def _():
        grad_tile(0, own_sib_flag, late_w.at[2:3], late_vn.at[2:3], dop, don, delta, qn, sib_ds, dsib_ref)


def last(qn, early_parts, late_w, late_vn, stats, scaled):
    outs = [((ROWS, 2 * DIM), BF16), ((ROWS, 2 * DIM), BF16), ((1, ROWS, COLS), BF16), ((1, ROWS, COLS), BF16)]
    operands = [qn, early_parts[0], early_parts[1], late_w, late_vn, stats, *scaled]
    return call(last_kernel, outs, operands, (), [], 6, 3_000_000_000)


def own_back_kernel(
    do_ref, own_ref, qn, w_ref, stats,
    near_ref, far_ref, near_sib_ref, far_sib_ref, own_sib_ref, near_ds, far_ds, near_sib_ds, sib_ds,
    dq_ref, dkv_ref,
    ds_own, don, dqacc,
):
    vn = own_ref[DIM : 2 * DIM, :].T
    for head in range(HEADS):
        cols = head_cols(head)
        low = slice(head * ROWS, head * ROWS + HALF)
        high = head_cols(head, HALF)
        scaled = (do_ref[head].astype(F32) * stats[32:33, cols]).astype(BF16)
        don[cols, :] = scaled.T
        dp_low = dot(vn[0:HALF], scaled[:, 0:HALF])
        dp_high = dot(vn, scaled[:, HALF:])
        ds_own[0:HALF, low] = (w_ref[0:HALF, low].astype(F32) * (dp_low - stats[40:41, low])).astype(BF16)
        ds_own[:, high] = (w_ref[:, high].astype(F32) * (dp_high - stats[40:41, high])).astype(BF16)
        dqacc[:, low] = dot(own_ref[0:DIM, 0:HALF], ds_own[0:HALF, low])
        dqacc[:, high] = dot(own_ref[0:DIM, :], ds_own[:, high])
    for part in range(2):
        span = slice(part * HALF, (part + 1) * HALF)
        dk = jnp.zeros((HALF, DIM), F32)
        dv = jnp.zeros((HALF, DIM), F32)
        for head in range(HEADS):
            cols = head_cols(head, part * HALF)
            dk = dk + dot(ds_own[span, cols], qn[cols, :])
            dv = dv + dot(w_ref[span, cols], don[cols, :])
        dkv_ref[span, :] = jnp.concatenate([dk, dv * (1.0 / SCALE)], axis=1).astype(BF16)

    tiles = (
        (near_ref.at[0:DIM], near_ds.at[0]),
        (far_ref.at[0:DIM], far_ds.at[0]),
        (near_sib_ref.at[0:DIM], near_sib_ds.at[0]),
        (far_sib_ref.at[0:DIM], sib_ds.at[0]),
        (own_sib_ref.at[0:DIM], sib_ds.at[0]),
    )
    for i, (kt, ds) in enumerate(tiles):
        @pl.when(read_flag(stats, 48 + i) > 0)
        def _():
            for head in range(HEADS):
                cols = head_cols(head)
                dqacc[:, cols] += dot(kt[...], ds[:, cols])

    for head in range(HEADS):
        dq_ref[head] = dqacc[:, head_cols(head)].astype(BF16)


def own_back(do, own, own_parts, stats, earlier, grad_scores):
    outs = [((HEADS, DIM, ROWS), BF16), ((ROWS, 2 * DIM), BF16)]
    scratch = [((ROWS, COLS), BF16), ((COLS, DIM), BF16), ((DIM, COLS), F32)]
    operands = [do, own, own_parts[1], own_parts[2], stats, *earlier, *grad_scores]
    return call(own_back_kernel, outs, operands, (), scratch, 8, 2_000_000_000)


def finish_kernel(*refs):
    total = refs[0][...].astype(F32)
    for ref in refs[1:-2]:
        total = total + ref[...].astype(F32)
    turned = total.T.astype(BF16)
    refs[-2][...] = turned[0:DIM]
    refs[-1][...] = turned[DIM:]


def finish(parts):
    shape = jax.ShapeDtypeStruct((DIM, PIECE), BF16)
    return pl.pallas_call(
        finish_kernel, out_shape=(shape, shape), in_specs=[VMEM] * len(parts), out_specs=(VMEM, VMEM),
        compiler_params=pltpu.CompilerParams(vmem_limit_bytes=4 * 1024 * 1024),
    )(*parts)


def shift(x, by):
    size = lax.axis_size("ctx")
    pairs = [(i, i + by) for i in range(size) if 0 <= i + by < size]
    return lax.ppermute(x, "ctx", pairs)


def swap(x):
    return lax.ppermute(x, "ctx", [(i, i ^ 1) for i in range(lax.axis_size("ctx"))])


def to_sibling(x, source):
    pairs = [(i, i ^ 1) for i in range(lax.axis_size("ctx")) if i % 2 == source]
    return lax.ppermute(x, "ctx", pairs)


def turn(x, by):
    return lax.ppermute(x, "tp", [(i, (i + by) % 4) for i in range(4)])


def local(queries, key_rows, values, grad_out, doc_ids):
    tp = lax.axis_index("tp")
    odd = lax.rem(lax.axis_index("ctx"), 2) == 1
    q = queries.transpose(1, 2, 0)
    do = grad_out.transpose(1, 2, 0)
    docs = jnp.broadcast_to((doc_ids + 1).astype(BF16)[None], (16, ROWS))
    own = jnp.concatenate([key_rows.T, values.T, docs], axis=0)
    starts = [lax.rem(tp + off, 4) * PIECE for off in OFFSETS]
    own, starts, odd = lax.optimization_barrier((own, starts, odd))
    zero = jnp.zeros((), starts[0].dtype)

    def home_slots(x):
        return [
            lax.dynamic_slice(x, (start, zero), (PIECE, 2 * DIM), allow_negative_indices=False) for start in starts
        ]

    near = shift(own, 2)
    far = shift(own, 4)
    own_parts = own_forward(q, own)
    near, far, own_parts = lax.optimization_barrier((near, far, own_parts))
    near_sib = swap(near)
    far_sib = to_sibling(far, 1)
    own_sib = to_sibling(own, 0)
    early_parts = early_forward(near, far, own, own_parts)
    near_sib, far_sib, own_sib, early_parts = lax.optimization_barrier((near_sib, far_sib, own_sib, early_parts))
    parts = middle(do, own, own_parts, early_parts, near_sib, far_sib, own_sib)
    attended, dnear, dnear_sib, near_ds, near_sib_ds, late_w, late_vn, stats = parts[:8]
    back = swap(dnear_sib)
    a1 = (dnear.astype(F32) + back.astype(F32)).astype(BF16)
    a1, stats = lax.optimization_barrier((a1, stats))
    a1_here = shift(a1, -2)
    dfar, dsib, far_ds, sib_ds = last(own_parts[1], early_parts, late_w, late_vn, stats, parts[8:])
    back = swap(dsib)
    a2 = (dfar.astype(F32) + jnp.where(odd, back.astype(F32), 0.0)).astype(BF16)
    a2 = home_slots(a2)
    a2, stats = lax.optimization_barrier((a2, stats))
    moved = [turn(a2[r], by) for r, by in RETURNS]
    earlier = (near, far, near_sib, far_sib, own_sib)
    dq, down = own_back(do, own, own_parts, stats, earlier, (near_ds, far_ds, near_sib_ds, sib_ds))
    moved, down = lax.optimization_barrier((moved, down))
    a2_sum = a2[0].astype(F32)
    for piece in moved:
        a2_sum = a2_sum + piece.astype(F32)
    a2_here = shift(a2_sum.astype(BF16), -4)
    a0 = down.astype(F32) + a1_here.astype(F32) + jnp.where(odd, 0.0, back.astype(F32))
    a0 = home_slots(a0.astype(BF16))
    parts = [a0[0], a2_here] + [turn(a0[r], by) for r, by in RETURNS]
    dk, dv = finish(parts)
    return attended.transpose(2, 0, 1), dq.transpose(2, 0, 1), dk.T, dv.T


def solution(mesh):
    placed = (P("ctx", "tp", None), P("ctx", None), P("ctx", None), P("ctx", "tp", None), P("ctx"))
    return jax.shard_map(
        local,
        mesh=mesh,
        in_specs=placed,
        out_specs=(
            P("ctx", "tp", None),
            P("ctx", "tp", None),
            P(("ctx", "tp"), None),
            P(("ctx", "tp"), None),
        ),
        check_vma=False,
    )
```

```python
import jax
import jax.numpy as jnp
from jax import lax
from jax.experimental import pallas as pl
from jax.experimental.pallas import tpu as pltpu
from jax.sharding import PartitionSpec as P

LOG2E = 1.4426950408889634
NEGATIVE = -1e30
ROWS = 512
HALF = 256
PIECE = 128
DIM = 192
WIDE = 256
DOC_ROW = 2 * DIM
PACKED = DOC_ROW + 16
HEADS = 3
COLS = HEADS * ROWS
SCALE = DIM ** -0.5
TO_LOG2 = SCALE * LOG2E
OFFSETS = (0, 3, 1, 2)
RETURNS = ((1, -1), (2, 1), (3, 2))
F32 = jnp.float32
BF16 = jnp.bfloat16
VMEM = pl.BlockSpec(memory_space=pltpu.VMEM)
SMEM = pl.BlockSpec(memory_space=pltpu.SMEM)


def dot(a, b):
    return jnp.dot(a, b, preferred_element_type=F32)


def head_cols(head, start=0):
    return slice(head * ROWS + start, (head + 1) * ROWS)


def one_hot(docs, width):
    rows = lax.broadcasted_iota(jnp.int32, (64, width), 0).astype(F32)
    return rows == docs.astype(F32)


def key_features(piece):
    hot = one_hot(piece[DOC_ROW : DOC_ROW + 1, :], piece.shape[1])
    return jnp.concatenate([piece[0:DIM, :], hot.astype(F32).astype(BF16)], axis=0).T


def folded(x):
    return x.reshape(x.shape[0] // 8, 8, x.shape[1])


def spread(row):
    return jnp.broadcast_to(row, (8, row.shape[1]))


def call(kernel, outs, operands, smem, scratch, limit, flops):
    return pl.pallas_call(
        kernel,
        out_shape=tuple(jax.ShapeDtypeStruct(shape, dtype) for shape, dtype in outs),
        in_specs=[SMEM if i in smem else VMEM for i in range(len(operands))],
        out_specs=tuple(SMEM if dtype == jnp.int32 else VMEM for _, dtype in outs),
        scratch_shapes=[pltpu.VMEM(shape, dtype) for shape, dtype in scratch],
        compiler_params=pltpu.CompilerParams(vmem_limit_bytes=limit * 1024 * 1024),
        cost_estimate=pl.CostEstimate(flops=flops, bytes_accessed=8_000_000, transcendentals=1_000_000),
    )(*operands)


def own_kernel(q_ref, own_ref, qe, qn, w_ref, top_ref, total_ref, o_ref):
    docs = own_ref[DOC_ROW : DOC_ROW + 1, :]
    mask_rows = jnp.where(one_hot(docs, ROWS), 0.0, NEGATIVE).astype(BF16)
    kn = key_features(own_ref[...])
    causal = lax.broadcasted_iota(jnp.int32, (HALF, HALF), 0) <= lax.broadcasted_iota(
        jnp.int32, (HALF, HALF), 1
    )
    for head in range(HEADS):
        cols = head_cols(head)
        low = slice(head * ROWS, head * ROWS + HALF)
        high = head_cols(head, HALF)
        qe[0:DIM, cols] = q_ref[head]
        qe[DIM:, cols] = mask_rows
        qn[cols, :] = q_ref[head].T
        s_low = jnp.where(causal, dot(kn[0:HALF], qe[:, low]), NEGATIVE)
        s_high = dot(kn, qe[:, high])
        s_top = s_high[0:HALF]
        s_last = jnp.where(causal, s_high[HALF:], NEGATIVE)
        for span, parts in ((low, (s_low,)), (high, (s_top, s_last))):
            peak = jnp.max(folded(parts[0]), axis=0)
            for s in parts[1:]:
                peak = jnp.maximum(peak, jnp.max(folded(s), axis=0))
            peak = spread(jnp.max(peak, axis=0, keepdims=True) * TO_LOG2)
            top_ref[:, span] = peak
            total = jnp.zeros((8, HALF), F32)
            for part, s in enumerate(parts):
                e = jnp.exp2(folded(s) * TO_LOG2 - peak[None])
                total = total + jnp.sum(e, axis=0)
                w_ref[part * HALF : (part + 1) * HALF, span] = e.reshape(HALF, HALF).astype(BF16)
            total_ref[:, span] = total
        o_ref[:, low] = dot(own_ref[DIM : 2 * DIM, 0:HALF], w_ref[0:HALF, low])
        o_ref[:, high] = dot(own_ref[DIM : 2 * DIM, :], w_ref[:, high])


def own_forward(q, own):
    outs = [
        ((WIDE, COLS), BF16), ((COLS, DIM), BF16), ((ROWS, COLS), BF16),
        ((8, COLS), F32), ((8, COLS), F32), ((DIM, COLS), F32),
    ]
    return call(own_kernel, outs, [q, own], (), [], 8, 800_000_000)


def needed_flag(rows, first_doc):
    matches = jnp.zeros((1, PIECE), F32)
    for row in rows:
        for start in range(0, row.shape[1], PIECE):
            docs = row[:, start : start + PIECE].astype(F32)
            matches = matches + jnp.where(docs == first_doc, 1.0, 0.0)
    return (jnp.max(matches) > 0.0).astype(jnp.int32)


def flag_row(flag):
    return jnp.broadcast_to(flag.astype(F32), (1, COLS))


def read_flag(ref, row):
    return (jnp.max(ref[row : row + 1, 0:PIECE]) > 0.0).astype(jnp.int32)


def score_pass(flags, tiles, kn, vts, qe, scores, w_ref, top0, total0, o0, top, total, o):
    top[...] = top0[...]

    for tile in range(tiles):
        @pl.when(flags[tile] > 0)
        def _():
            for head in range(HEADS):
                cols = head_cols(head)
                s = dot(kn[tile], qe[:, cols]) * TO_LOG2
                scores[tile, :, cols] = s
                top[:, cols] = jnp.maximum(top[:, cols], jnp.max(folded(s), axis=0))

    top[...] = spread(jnp.max(top[...], axis=0, keepdims=True))
    shrink = jnp.exp2(top0[...] - top[...])
    total[...] = total0[...] * shrink
    for head in range(HEADS):
        cols = head_cols(head)
        o[:, cols] = o0[:, cols] * shrink[0:1, cols]

    for tile in range(tiles):
        @pl.when(flags[tile] > 0)
        def _():
            for head in range(HEADS):
                cols = head_cols(head)
                e = jnp.exp2(folded(scores[tile, :, cols]) - top[:, cols][None])
                total[:, cols] += jnp.sum(e, axis=0)
                w = e.reshape(ROWS, ROWS).astype(BF16)
                w_ref[tile, :, cols] = w
                o[:, cols] += dot(vts[tile](), w)


def prepare(refs, own_ref, kn, vn):
    first_doc = own_ref[DOC_ROW : DOC_ROW + 1, 0:1].astype(F32)
    flags = [needed_flag([ref[DOC_ROW : DOC_ROW + 1, :]], first_doc) for ref in refs]
    for tile, ref in enumerate(refs):
        @pl.when(flags[tile] > 0)
        def _():
            kn[tile] = key_features(ref[...])
            vn[tile] = ref[DIM : 2 * DIM, :].T
    return flags


def early_kernel(
    near_ref, far_ref, own_ref, qe, top0, total0, o0,
    w_ref, vn, top, total, o, flag_ref,
    kn, scores,
):
    refs = (near_ref, far_ref)
    flags = prepare(refs, own_ref, kn, vn)
    for tile in range(2):
        flag_ref[tile : tile + 1, :] = flag_row(flags[tile])
    vts = [lambda ref=ref: ref[DIM : 2 * DIM, :] for ref in refs]
    score_pass(flags, 2, kn, vts, qe, scores, w_ref, top0, total0, o0, top, total, o)


def early_forward(near, far, own, own_parts):
    qe, _, _, top, total, o = own_parts
    outs = [
        ((2, ROWS, COLS), BF16), ((2, ROWS, DIM), BF16),
        ((8, COLS), F32), ((8, COLS), F32), ((DIM, COLS), F32), ((8, COLS), F32),
    ]
    scratch = [((2, ROWS, WIDE), BF16), ((2, ROWS, COLS), F32)]
    operands = [near, far, own, qe, top, total, o]
    return call(early_kernel, outs, operands, (), scratch, 12, 3_000_000_000)


def grad_tile(tile, flag, w, vn, dop, don, delta, qn, ds_ref, out):
    @pl.when(flag > 0)
    def _():
        for head in range(HEADS):
            cols = head_cols(head)
            dp = folded(dot(vn[tile], dop[:, cols]))
            wide = folded(w[tile, :, cols].astype(F32))
            ds = (wide * (dp - delta[:, cols][None])).reshape(ROWS, ROWS)
            ds_ref[tile, :, cols] = ds.astype(BF16)
        dk = dot(ds_ref[tile], qn[...])
        dv = dot(w[tile], don[...])
        out[...] = jnp.concatenate([dk, dv * (1.0 / SCALE)], axis=1).astype(BF16)

    @pl.when(flag == 0)
    def _():
        out[...] = jnp.zeros((ROWS, 2 * DIM), BF16)


def scaled_grads(do_ref, ratio, dop, don):
    for head in range(HEADS):
        cols = head_cols(head)
        scaled = (do_ref[head].astype(F32) * ratio[0:1, cols]).astype(BF16)
        dop[:, cols] = scaled
        don[cols, :] = scaled.T


def middle_kernel(
    early_flag_ref, do_ref, own_ref, qe, qn, top_own, early_w, early_vn, top_early, total_early, o_early,
    near_sib_ref, far_sib_ref, own_sib_ref,
    o_ref, dnear_ref, dnear_sib_ref, near_ds, near_sib_ds, late_w, late_vn, stats, dop_early, don_early, dop, don,
    kn, scores, top, total, o,
):
    refs = (near_sib_ref, far_sib_ref, own_sib_ref)
    late_flags = prepare(refs, own_ref, kn, late_vn)
    early_flags = [read_flag(early_flag_ref, tile) for tile in range(2)]
    for i, flag in enumerate(early_flags + late_flags):
        stats[48 + i : 49 + i, :] = flag_row(flag)
    vts = [lambda ref=ref: ref[DIM : 2 * DIM, :] for ref in refs]
    score_pass(late_flags, 3, kn, vts, qe, scores, late_w, top_early, total_early, o_early, top, total, o)

    early_shrink = jnp.exp2(top_early[...] - top[...])
    own_shrink = jnp.exp2(top_own[...] - top[...])
    for head in range(HEADS):
        cols = head_cols(head)
        inverse = 1.0 / jnp.sum(total[:, cols], axis=0, keepdims=True)
        attended = (o[:, cols] * inverse).astype(BF16)
        o_ref[head] = attended
        delta = jnp.sum(do_ref[head].astype(F32) * attended.astype(F32), axis=0, keepdims=True)
        ratio = spread(inverse * SCALE)
        for i, shrink in enumerate((None, early_shrink, own_shrink)):
            part = ratio if shrink is None else ratio * shrink[:, cols]
            stats[i * 16 : i * 16 + 8, cols] = part
            stats[i * 16 + 8 : i * 16 + 16, cols] = part * delta

    scaled_grads(do_ref, stats.at[16:24], dop_early, don_early)
    scaled_grads(do_ref, stats.at[0:8], dop, don)
    grad_tile(0, early_flags[0], early_w, early_vn, dop_early, don_early, stats.at[24:32], qn, near_ds, dnear_ref)
    grad_tile(0, late_flags[0], late_w, late_vn, dop, don, stats.at[8:16], qn, near_sib_ds, dnear_sib_ref)


def middle(do, own, own_parts, early_parts, near_sib, far_sib, own_sib):
    qe, qn, _, top_own, _, _ = own_parts
    early_w, early_vn, top, total, o, flags = early_parts
    outs = [
        ((HEADS, DIM, ROWS), BF16), ((ROWS, 2 * DIM), BF16), ((ROWS, 2 * DIM), BF16),
        ((1, ROWS, COLS), BF16), ((1, ROWS, COLS), BF16),
        ((3, ROWS, COLS), BF16), ((3, ROWS, DIM), BF16), ((56, COLS), F32),
        ((DIM, COLS), BF16), ((COLS, DIM), BF16), ((DIM, COLS), BF16), ((COLS, DIM), BF16),
    ]
    scratch = [
        ((3, ROWS, WIDE), BF16), ((3, ROWS, COLS), F32),
        ((8, COLS), F32), ((8, COLS), F32), ((DIM, COLS), F32),
    ]
    operands = [
        flags, do, own, qe, qn, top_own, early_w, early_vn, top, total, o, near_sib, far_sib, own_sib
    ]
    return call(middle_kernel, outs, operands, (), scratch, 18, 5_000_000_000)


def last_kernel(
    qn, early_w, early_vn, late_w, late_vn, stats, dop_early, don_early, dop, don,
    dfar_ref, dsib_ref, far_ds, sib_ds,
):
    early_delta = stats.at[24:32]
    delta = stats.at[8:16]
    grad_tile(
        0, read_flag(stats, 49), early_w.at[1:2], early_vn.at[1:2], dop_early, don_early, early_delta, qn, far_ds,
        dfar_ref,
    )
    own_sib_flag = read_flag(stats, 52)
    grad_tile(0, read_flag(stats, 51), late_w.at[1:2], late_vn.at[1:2], dop, don, delta, qn, sib_ds, dsib_ref)

    @pl.when(own_sib_flag > 0)
    def _():
        grad_tile(0, own_sib_flag, late_w.at[2:3], late_vn.at[2:3], dop, don, delta, qn, sib_ds, dsib_ref)


def last(qn, early_parts, late_w, late_vn, stats, scaled):
    outs = [((ROWS, 2 * DIM), BF16), ((ROWS, 2 * DIM), BF16), ((1, ROWS, COLS), BF16), ((1, ROWS, COLS), BF16)]
    operands = [qn, early_parts[0], early_parts[1], late_w, late_vn, stats, *scaled]
    return call(last_kernel, outs, operands, (), [], 6, 3_000_000_000)


def own_back_kernel(
    do_ref, own_ref, qn, w_ref, stats,
    dkv_ref, ds_own,
    don,
):
    vn = own_ref[DIM : 2 * DIM, :].T
    for head in range(HEADS):
        cols = head_cols(head)
        low = slice(head * ROWS, head * ROWS + HALF)
        high = head_cols(head, HALF)
        scaled = (do_ref[head].astype(F32) * stats[32:33, cols]).astype(BF16)
        don[cols, :] = scaled.T
        dp_low = dot(vn[0:HALF], scaled[:, 0:HALF])
        dp_high = dot(vn, scaled[:, HALF:])
        ds_own[0:HALF, low] = (w_ref[0:HALF, low].astype(F32) * (dp_low - stats[40:41, low])).astype(BF16)
        ds_own[:, high] = (w_ref[:, high].astype(F32) * (dp_high - stats[40:41, high])).astype(BF16)
    for part in range(2):
        span = slice(part * HALF, (part + 1) * HALF)
        dk = jnp.zeros((HALF, DIM), F32)
        dv = jnp.zeros((HALF, DIM), F32)
        for head in range(HEADS):
            cols = head_cols(head, part * HALF)
            dk = dk + dot(ds_own[span, cols], qn[cols, :])
            dv = dv + dot(w_ref[span, cols], don[cols, :])
        dkv_ref[span, :] = jnp.concatenate([dk, dv * (1.0 / SCALE)], axis=1).astype(BF16)


def query_grad_kernel(
    own_ref, stats, near_ref, far_ref, near_sib_ref, far_sib_ref, own_sib_ref,
    own_ds, near_ds, far_ds, near_sib_ds, sib_ds,
    dq_ref,
    dqacc,
):
    for head in range(HEADS):
        low = slice(head * ROWS, head * ROWS + HALF)
        high = head_cols(head, HALF)
        dqacc[:, low] = dot(own_ref[0:DIM, 0:HALF], own_ds[0:HALF, low])
        dqacc[:, high] = dot(own_ref[0:DIM, :], own_ds[:, high])

    tiles = (
        (near_ref.at[0:DIM], near_ds.at[0]),
        (far_ref.at[0:DIM], far_ds.at[0]),
        (near_sib_ref.at[0:DIM], near_sib_ds.at[0]),
        (far_sib_ref.at[0:DIM], sib_ds.at[0]),
        (own_sib_ref.at[0:DIM], sib_ds.at[0]),
    )
    for i, (kt, ds) in enumerate(tiles):
        @pl.when(read_flag(stats, 48 + i) > 0)
        def _():
            for head in range(HEADS):
                cols = head_cols(head)
                dqacc[:, cols] += dot(kt[...], ds[:, cols])

    for head in range(HEADS):
        dq_ref[head] = dqacc[:, head_cols(head)].astype(BF16)


def own_back(do, own, own_parts, stats):
    outs = [((ROWS, 2 * DIM), BF16), ((ROWS, COLS), BF16)]
    operands = [do, own, own_parts[1], own_parts[2], stats]
    return call(own_back_kernel, outs, operands, (), [((COLS, DIM), BF16)], 6, 1_000_000_000)


def query_grad(own, stats, earlier, grad_scores):
    outs = [((HEADS, DIM, ROWS), BF16)]
    operands = [own, stats, *earlier, *grad_scores]
    return call(query_grad_kernel, outs, operands, (), [((DIM, COLS), F32)], 6, 1_000_000_000)[0]


def finish_kernel(*refs):
    total = refs[0][...].astype(F32)
    for ref in refs[1:-2]:
        total = total + ref[...].astype(F32)
    turned = total.T.astype(BF16)
    refs[-2][...] = turned[0:DIM]
    refs[-1][...] = turned[DIM:]


def finish(parts):
    shape = jax.ShapeDtypeStruct((DIM, PIECE), BF16)
    return pl.pallas_call(
        finish_kernel, out_shape=(shape, shape), in_specs=[VMEM] * len(parts), out_specs=(VMEM, VMEM),
        compiler_params=pltpu.CompilerParams(vmem_limit_bytes=4 * 1024 * 1024),
    )(*parts)


def shift(x, by):
    size = lax.axis_size("ctx")
    pairs = [(i, i + by) for i in range(size) if 0 <= i + by < size]
    return lax.ppermute(x, "ctx", pairs)


def swap(x):
    return lax.ppermute(x, "ctx", [(i, i ^ 1) for i in range(lax.axis_size("ctx"))])


def to_sibling(x, source):
    pairs = [(i, i ^ 1) for i in range(lax.axis_size("ctx")) if i % 2 == source]
    return lax.ppermute(x, "ctx", pairs)


def turn(x, by):
    return lax.ppermute(x, "tp", [(i, (i + by) % 4) for i in range(4)])


def local(queries, key_rows, values, grad_out, doc_ids):
    tp = lax.axis_index("tp")
    odd = lax.rem(lax.axis_index("ctx"), 2) == 1
    q = queries.transpose(1, 2, 0)
    do = grad_out.transpose(1, 2, 0)
    docs = jnp.broadcast_to((doc_ids + 1).astype(BF16)[None], (16, ROWS))
    own = jnp.concatenate([key_rows.T, values.T, docs], axis=0)
    starts = [lax.rem(tp + off, 4) * PIECE for off in OFFSETS]
    half = lax.rem(tp, 2) * HALF
    far_starts = [lax.rem(start + half, ROWS) for start in starts]
    own, starts, far_starts, half, odd = lax.optimization_barrier((own, starts, far_starts, half, odd))
    zero = jnp.zeros((), starts[0].dtype)

    def home_slots(x, starts):
        return [
            lax.dynamic_slice(x, (start, zero), (PIECE, 2 * DIM), allow_negative_indices=False) for start in starts
        ]

    far = shift(lax.dynamic_slice(own, (zero, half), (PACKED, HALF), allow_negative_indices=False), 4)
    near = shift(own, 2)
    far = jnp.concatenate([far, lax.ppermute(far, "tp", [(i, i ^ 1) for i in range(4)])], axis=1)
    own_parts = own_forward(q, own)
    near, far, own_parts = lax.optimization_barrier((near, far, own_parts))
    near_sib = swap(near)
    far_sib = to_sibling(far, 1)
    own_sib = to_sibling(own, 0)
    early_parts = early_forward(near, far, own, own_parts)
    near_sib, far_sib, own_sib, early_parts = lax.optimization_barrier((near_sib, far_sib, own_sib, early_parts))
    parts = middle(do, own, own_parts, early_parts, near_sib, far_sib, own_sib)
    attended, dnear, dnear_sib, near_ds, near_sib_ds, late_w, late_vn, stats = parts[:8]
    back = swap(dnear_sib)
    a1 = (dnear.astype(F32) + back.astype(F32)).astype(BF16)
    a1_here = shift(a1, -2)
    dfar, dsib, far_ds, sib_ds = last(own_parts[1], early_parts, late_w, late_vn, stats, parts[8:])
    back = swap(dsib)
    a2 = (dfar.astype(F32) + jnp.where(odd, back.astype(F32), 0.0)).astype(BF16)
    a2 = home_slots(a2, far_starts)
    a2, stats = lax.optimization_barrier((a2, stats))
    moved = [turn(a2[r], by) for r, by in RETURNS]
    down, own_ds = own_back(do, own, own_parts, stats)
    moved, down = lax.optimization_barrier((moved, down))
    a2_sum = a2[0].astype(F32)
    for piece in moved:
        a2_sum = a2_sum + piece.astype(F32)
    a2_here = shift(a2_sum.astype(BF16), -4)
    a0 = down.astype(F32) + a1_here.astype(F32) + jnp.where(odd, 0.0, back.astype(F32))
    a0 = home_slots(a0.astype(BF16), starts)
    a0, own_ds = lax.optimization_barrier((a0, own_ds))
    parts = [a0[0], a2_here] + [turn(a0[r], by) for r, by in RETURNS]
    earlier = (near, far, near_sib, far_sib, own_sib)
    dq = query_grad(own, stats, earlier, (own_ds, near_ds, far_ds, near_sib_ds, sib_ds))
    dk, dv = finish(parts)
    return attended.transpose(2, 0, 1), dq.transpose(2, 0, 1), dk.T, dv.T


def solution(mesh):
    placed = (P("ctx", "tp", None), P("ctx", None), P("ctx", None), P("ctx", "tp", None), P("ctx"))
    return jax.shard_map(
        local,
        mesh=mesh,
        in_specs=placed,
        out_specs=(
            P("ctx", "tp", None),
            P("ctx", "tp", None),
            P(("ctx", "tp"), None),
            P(("ctx", "tp"), None),
        ),
        check_vma=False,
    )
```

```python
import jax
import jax.numpy as jnp
from jax import lax
from jax.experimental import pallas as pl
from jax.experimental.pallas import tpu as pltpu
from jax.sharding import PartitionSpec as P

LOG2E = 1.4426950408889634
NEGATIVE = -1e30
ROWS = 512
HALF = 256
PIECE = 128
DIM = 192
WIDE = 256
DOC_ROW = 2 * DIM
PACKED = DOC_ROW + 16
HEADS = 3
COLS = HEADS * ROWS
SCALE = DIM ** -0.5
TO_LOG2 = SCALE * LOG2E
OFFSETS = (0, 3, 1, 2)
RETURNS = ((1, -1), (2, 1), (3, 2))
F32 = jnp.float32
BF16 = jnp.bfloat16
VMEM = pl.BlockSpec(memory_space=pltpu.VMEM)
SMEM = pl.BlockSpec(memory_space=pltpu.SMEM)


def dot(a, b):
    return jnp.dot(a, b, preferred_element_type=F32)


def head_cols(head, start=0):
    return slice(head * ROWS + start, (head + 1) * ROWS)


def one_hot(docs, width):
    rows = lax.broadcasted_iota(jnp.int32, (64, width), 0).astype(F32)
    return rows == docs.astype(F32)


def key_features(piece):
    hot = one_hot(piece[DOC_ROW : DOC_ROW + 1, :], piece.shape[1])
    return jnp.concatenate([piece[0:DIM, :], hot.astype(F32).astype(BF16)], axis=0).T


def folded(x):
    return x.reshape(x.shape[0] // 8, 8, x.shape[1])


def spread(row):
    return jnp.broadcast_to(row, (8, row.shape[1]))


def call(kernel, outs, operands, smem, scratch, limit, flops):
    return pl.pallas_call(
        kernel,
        out_shape=tuple(jax.ShapeDtypeStruct(shape, dtype) for shape, dtype in outs),
        in_specs=[SMEM if i in smem else VMEM for i in range(len(operands))],
        out_specs=tuple(SMEM if dtype == jnp.int32 else VMEM for _, dtype in outs),
        scratch_shapes=[pltpu.VMEM(shape, dtype) for shape, dtype in scratch],
        compiler_params=pltpu.CompilerParams(vmem_limit_bytes=limit * 1024 * 1024),
        cost_estimate=pl.CostEstimate(flops=flops, bytes_accessed=8_000_000, transcendentals=1_000_000),
    )(*operands)


def own_kernel(q_ref, own_ref, qe, qn, w_ref, top_ref, total_ref, o_ref):
    docs = own_ref[DOC_ROW : DOC_ROW + 1, :]
    mask_rows = jnp.where(one_hot(docs, ROWS), 0.0, NEGATIVE).astype(BF16)
    kn = key_features(own_ref[...])
    causal = lax.broadcasted_iota(jnp.int32, (HALF, HALF), 0) <= lax.broadcasted_iota(
        jnp.int32, (HALF, HALF), 1
    )
    for head in range(HEADS):
        cols = head_cols(head)
        low = slice(head * ROWS, head * ROWS + HALF)
        high = head_cols(head, HALF)
        qe[0:DIM, cols] = q_ref[head]
        qe[DIM:, cols] = mask_rows
        qn[cols, :] = q_ref[head].T
        s_low = jnp.where(causal, dot(kn[0:HALF], qe[:, low]), NEGATIVE)
        s_high = dot(kn, qe[:, high])
        s_top = s_high[0:HALF]
        s_last = jnp.where(causal, s_high[HALF:], NEGATIVE)
        for span, parts in ((low, (s_low,)), (high, (s_top, s_last))):
            peak = jnp.max(folded(parts[0]), axis=0)
            for s in parts[1:]:
                peak = jnp.maximum(peak, jnp.max(folded(s), axis=0))
            peak = spread(jnp.max(peak, axis=0, keepdims=True) * TO_LOG2)
            top_ref[:, span] = peak
            total = jnp.zeros((8, HALF), F32)
            for part, s in enumerate(parts):
                e = jnp.exp2(folded(s) * TO_LOG2 - peak[None])
                total = total + jnp.sum(e, axis=0)
                w_ref[part * HALF : (part + 1) * HALF, span] = e.reshape(HALF, HALF).astype(BF16)
            total_ref[:, span] = total
        o_ref[:, low] = dot(own_ref[DIM : 2 * DIM, 0:HALF], w_ref[0:HALF, low])
        o_ref[:, high] = dot(own_ref[DIM : 2 * DIM, :], w_ref[:, high])


def own_forward(q, own):
    outs = [
        ((WIDE, COLS), BF16), ((COLS, DIM), BF16), ((ROWS, COLS), BF16),
        ((8, COLS), F32), ((8, COLS), F32), ((DIM, COLS), F32),
    ]
    return call(own_kernel, outs, [q, own], (), [], 8, 800_000_000)


def needed_flag(rows, first_doc):
    matches = jnp.zeros((1, PIECE), F32)
    for row in rows:
        for start in range(0, row.shape[1], PIECE):
            docs = row[:, start : start + PIECE].astype(F32)
            matches = matches + jnp.where(docs == first_doc, 1.0, 0.0)
    return (jnp.max(matches) > 0.0).astype(jnp.int32)


def flag_row(flag):
    return jnp.broadcast_to(flag.astype(F32), (1, COLS))


def read_flag(ref, row):
    return (jnp.max(ref[row : row + 1, 0:PIECE]) > 0.0).astype(jnp.int32)


def whole(tile, flag):
    return (flag, tile, slice(0, ROWS), ROWS)


def far_blocks(tile, flags):
    narrow, low, high = flags
    return [
        (narrow, tile, slice(0, ROWS), HALF),
        (low, tile, slice(0, HALF), ROWS),
        (high, tile, slice(HALF, ROWS), ROWS),
    ]


def block_cols(head, width):
    return slice(head * ROWS, head * ROWS + width)


def score_pass(blocks, kn, vts, qe, scores, w_ref, top0, total0, o0, top, total, o):
    top[...] = top0[...]

    for flag, tile, rows, width in blocks:
        @pl.when(flag > 0)
        def _():
            for head in range(HEADS):
                cols = block_cols(head, width)
                s = dot(kn[tile, rows], qe[:, cols]) * TO_LOG2
                scores[tile, rows, cols] = s
                top[:, cols] = jnp.maximum(top[:, cols], jnp.max(folded(s), axis=0))

    top[...] = spread(jnp.max(top[...], axis=0, keepdims=True))
    shrink = jnp.exp2(top0[...] - top[...])
    total[...] = total0[...] * shrink
    for head in range(HEADS):
        cols = head_cols(head)
        o[:, cols] = o0[:, cols] * shrink[0:1, cols]

    for flag, tile, rows, width in blocks:
        @pl.when(flag > 0)
        def _():
            for head in range(HEADS):
                cols = block_cols(head, width)
                e = jnp.exp2(folded(scores[tile, rows, cols]) - top[:, cols][None])
                total[:, cols] += jnp.sum(e, axis=0)
                w = e.reshape(rows.stop - rows.start, width).astype(BF16)
                w_ref[tile, rows, cols] = w
                o[:, cols] += dot(vts[tile](rows), w)


def prepare(refs, own_ref, kn, vn):
    first_doc = own_ref[DOC_ROW : DOC_ROW + 1, 0:1].astype(F32)
    flags = [needed_flag([ref[DOC_ROW : DOC_ROW + 1, :]], first_doc) for ref in refs]
    for tile, ref in enumerate(refs):
        @pl.when(flags[tile] > 0)
        def _():
            kn[tile] = key_features(ref[...])
            vn[tile] = ref[DIM : 2 * DIM, :].T
    return flags


def early_kernel(
    near_ref, far_ref, own_ref, qe, top0, total0, o0,
    w_ref, vn, top, total, o, flag_ref,
    kn, scores,
):
    refs = (near_ref, far_ref)
    near_flag, far_flag = prepare(refs, own_ref, kn, vn)
    own_docs = own_ref[DOC_ROW : DOC_ROW + 1, :].astype(F32)
    first_doc = own_docs[:, 0:1]
    is_narrow = 1 - needed_flag([own_docs[:, HALF:]], first_doc)
    halves = [needed_flag([far_ref[DOC_ROW : DOC_ROW + 1, span]], first_doc) for span in (slice(0, HALF), slice(HALF, ROWS))]
    far_flags = [far_flag * is_narrow] + [half * (1 - is_narrow) for half in halves]
    for i, flag in enumerate([near_flag] + far_flags):
        flag_ref[i : i + 1, :] = flag_row(flag)
    vts = [lambda rows, ref=ref: ref[DIM : 2 * DIM, rows] for ref in refs]
    score_pass([whole(0, near_flag)] + far_blocks(1, far_flags), kn, vts, qe, scores, w_ref, top0, total0, o0, top, total, o)


def early_forward(near, far, own, own_parts):
    qe, _, _, top, total, o = own_parts
    outs = [
        ((2, ROWS, COLS), BF16), ((2, ROWS, DIM), BF16),
        ((8, COLS), F32), ((8, COLS), F32), ((DIM, COLS), F32), ((8, COLS), F32),
    ]
    scratch = [((2, ROWS, WIDE), BF16), ((2, ROWS, COLS), F32)]
    operands = [near, far, own, qe, top, total, o]
    return call(early_kernel, outs, operands, (), scratch, 12, 3_000_000_000)


def grad_tile(blocks, w, vn, dop, don, delta, qn, ds_ref, out):
    @pl.when(blocks[0][0] == 0)
    def _():
        out[...] = jnp.zeros((ROWS, 2 * DIM), BF16)

    for flag, tile, rows, width in blocks:
        @pl.when(flag > 0)
        def _():
            count = rows.stop - rows.start
            for head in range(HEADS):
                cols = block_cols(head, width)
                dp = folded(dot(vn[tile, rows], dop[:, cols]))
                wide = folded(w[tile, rows, cols].astype(F32))
                ds = (wide * (dp - delta[:, cols][None])).reshape(count, width)
                ds_ref[0, rows, cols] = ds.astype(BF16)
            if width == ROWS:
                dk = dot(ds_ref[0, rows], qn[...])
                dv = dot(w[tile, rows], don[...])
            else:
                spans = [block_cols(head, width) for head in range(HEADS)]
                dk = sum(dot(ds_ref[0, rows, cols], qn[cols, :]) for cols in spans)
                dv = sum(dot(w[tile, rows, cols], don[cols, :]) for cols in spans)
            out[rows] = jnp.concatenate([dk, dv * (1.0 / SCALE)], axis=1).astype(BF16)


def scaled_grads(do_ref, ratio, dop, don):
    for head in range(HEADS):
        cols = head_cols(head)
        scaled = (do_ref[head].astype(F32) * ratio[0:1, cols]).astype(BF16)
        dop[:, cols] = scaled
        don[cols, :] = scaled.T


def middle_kernel(
    early_flag_ref, do_ref, own_ref, qe, qn, top_own, early_w, early_vn, top_early, total_early, o_early,
    near_sib_ref, far_sib_ref, own_sib_ref,
    o_ref, dnear_ref, dnear_sib_ref, near_ds, near_sib_ds, late_w, late_vn, stats, dop_early, don_early, dop, don,
    kn, scores, top, total, o,
):
    refs = (near_sib_ref, far_sib_ref, own_sib_ref)
    late_flags = prepare(refs, own_ref, kn, late_vn)
    early_flags = [read_flag(early_flag_ref, i) for i in range(4)]
    for i, flag in enumerate(early_flags + late_flags):
        stats[48 + i : 49 + i, :] = flag_row(flag)
    vts = [lambda rows, ref=ref: ref[DIM : 2 * DIM, rows] for ref in refs]
    score_pass([whole(tile, flag) for tile, flag in enumerate(late_flags)], kn, vts, qe, scores, late_w, top_early, total_early, o_early, top, total, o)

    early_shrink = jnp.exp2(top_early[...] - top[...])
    own_shrink = jnp.exp2(top_own[...] - top[...])
    for head in range(HEADS):
        cols = head_cols(head)
        inverse = 1.0 / jnp.sum(total[:, cols], axis=0, keepdims=True)
        attended = (o[:, cols] * inverse).astype(BF16)
        o_ref[head] = attended
        delta = jnp.sum(do_ref[head].astype(F32) * attended.astype(F32), axis=0, keepdims=True)
        ratio = spread(inverse * SCALE)
        for i, shrink in enumerate((None, early_shrink, own_shrink)):
            part = ratio if shrink is None else ratio * shrink[:, cols]
            stats[i * 16 : i * 16 + 8, cols] = part
            stats[i * 16 + 8 : i * 16 + 16, cols] = part * delta

    scaled_grads(do_ref, stats.at[16:24], dop_early, don_early)
    scaled_grads(do_ref, stats.at[0:8], dop, don)
    early_delta = stats.at[24:32]
    grad_tile([whole(0, early_flags[0])], early_w, early_vn, dop_early, don_early, early_delta, qn, near_ds, dnear_ref)
    grad_tile([whole(0, late_flags[0])], late_w, late_vn, dop, don, stats.at[8:16], qn, near_sib_ds, dnear_sib_ref)


def middle(do, own, own_parts, early_parts, near_sib, far_sib, own_sib):
    qe, qn, _, top_own, _, _ = own_parts
    early_w, early_vn, top, total, o, flags = early_parts
    outs = [
        ((HEADS, DIM, ROWS), BF16), ((ROWS, 2 * DIM), BF16), ((ROWS, 2 * DIM), BF16),
        ((1, ROWS, COLS), BF16), ((1, ROWS, COLS), BF16),
        ((3, ROWS, COLS), BF16), ((3, ROWS, DIM), BF16), ((56, COLS), F32),
        ((DIM, COLS), BF16), ((COLS, DIM), BF16), ((DIM, COLS), BF16), ((COLS, DIM), BF16),
    ]
    scratch = [
        ((3, ROWS, WIDE), BF16), ((3, ROWS, COLS), F32),
        ((8, COLS), F32), ((8, COLS), F32), ((DIM, COLS), F32),
    ]
    operands = [
        flags, do, own, qe, qn, top_own, early_w, early_vn, top, total, o, near_sib, far_sib, own_sib
    ]
    return call(middle_kernel, outs, operands, (), scratch, 18, 5_000_000_000)


def last_kernel(
    qn, early_w, early_vn, late_w, late_vn, stats, dop_early, don_early, dop, don,
    dfar_ref, dsib_ref, far_ds, sib_ds,
):
    early_delta = stats.at[24:32]
    delta = stats.at[8:16]
    far_flags = [read_flag(stats, 49 + i) for i in range(3)]
    grad_tile(
        far_blocks(1, far_flags), early_w, early_vn, dop_early, don_early, early_delta, qn, far_ds, dfar_ref
    )
    own_sib_flag = read_flag(stats, 54)
    grad_tile([whole(1, read_flag(stats, 53))], late_w, late_vn, dop, don, delta, qn, sib_ds, dsib_ref)

    @pl.when(own_sib_flag > 0)
    def _():
        grad_tile([whole(2, own_sib_flag)], late_w, late_vn, dop, don, delta, qn, sib_ds, dsib_ref)


def last(qn, early_parts, late_w, late_vn, stats, scaled):
    outs = [((ROWS, 2 * DIM), BF16), ((ROWS, 2 * DIM), BF16), ((1, ROWS, COLS), BF16), ((1, ROWS, COLS), BF16)]
    operands = [qn, early_parts[0], early_parts[1], late_w, late_vn, stats, *scaled]
    return call(last_kernel, outs, operands, (), [], 6, 3_000_000_000)


def own_back_kernel(
    do_ref, own_ref, qn, w_ref, stats, near_ref, near_sib_ref, near_ds, near_sib_ds,
    dkv_ref, ds_own, dq_part,
    don,
):
    vn = own_ref[DIM : 2 * DIM, :].T
    for head in range(HEADS):
        cols = head_cols(head)
        low = slice(head * ROWS, head * ROWS + HALF)
        high = head_cols(head, HALF)
        scaled = (do_ref[head].astype(F32) * stats[32:33, cols]).astype(BF16)
        don[cols, :] = scaled.T
        dp_low = dot(vn[0:HALF], scaled[:, 0:HALF])
        dp_high = dot(vn, scaled[:, HALF:])
        ds_own[0:HALF, low] = (w_ref[0:HALF, low].astype(F32) * (dp_low - stats[40:41, low])).astype(BF16)
        ds_own[:, high] = (w_ref[:, high].astype(F32) * (dp_high - stats[40:41, high])).astype(BF16)
    for part in range(2):
        span = slice(part * HALF, (part + 1) * HALF)
        dk = jnp.zeros((HALF, DIM), F32)
        dv = jnp.zeros((HALF, DIM), F32)
        for head in range(HEADS):
            cols = head_cols(head, part * HALF)
            dk = dk + dot(ds_own[span, cols], qn[cols, :])
            dv = dv + dot(w_ref[span, cols], don[cols, :])
        dkv_ref[span, :] = jnp.concatenate([dk, dv * (1.0 / SCALE)], axis=1).astype(BF16)

    for head in range(HEADS):
        low = slice(head * ROWS, head * ROWS + HALF)
        high = head_cols(head, HALF)
        dq_part[:, low] = dot(own_ref[0:DIM, 0:HALF], ds_own[0:HALF, low])
        dq_part[:, high] = dot(own_ref[0:DIM, :], ds_own[:, high])
    query_terms(
        [(whole(0, read_flag(stats, 48)), near_ref, near_ds), (whole(0, read_flag(stats, 52)), near_sib_ref, near_sib_ds)],
        dq_part,
    )


def query_terms(terms, total):
    for (flag, _, rows, width), kt, ds in terms:
        @pl.when(flag > 0)
        def _():
            for head in range(HEADS):
                cols = block_cols(head, width)
                total[:, cols] += dot(kt[0:DIM, rows], ds[0, rows, cols])


def query_grad_kernel(
    dq_part, stats, far_ref, far_sib_ref, own_sib_ref, far_ds, sib_ds,
    dq_ref,
    total,
):
    total[...] = dq_part[...]
    far_flags = [read_flag(stats, 49 + i) for i in range(3)]
    terms = [(block, far_ref, far_ds) for block in far_blocks(0, far_flags)]
    terms.append((whole(0, read_flag(stats, 53)), far_sib_ref, sib_ds))
    terms.append((whole(0, read_flag(stats, 54)), own_sib_ref, sib_ds))
    query_terms(terms, total)
    for head in range(HEADS):
        dq_ref[head] = total[:, head_cols(head)].astype(BF16)


def own_back(do, own, own_parts, stats, near, near_sib, near_ds, near_sib_ds):
    outs = [((ROWS, 2 * DIM), BF16), ((ROWS, COLS), BF16), ((DIM, COLS), F32)]
    operands = [do, own, own_parts[1], own_parts[2], stats, near, near_sib, near_ds, near_sib_ds]
    return call(own_back_kernel, outs, operands, (), [((COLS, DIM), BF16)], 6, 1_000_000_000)


def query_grad(dq_part, stats, far, far_sib, own_sib, far_ds, sib_ds):
    outs = [((HEADS, DIM, ROWS), BF16)]
    operands = [dq_part, stats, far, far_sib, own_sib, far_ds, sib_ds]
    return call(query_grad_kernel, outs, operands, (), [((DIM, COLS), F32)], 6, 1_000_000_000)[0]


def finish_kernel(*refs):
    total = refs[0][...].astype(F32)
    for ref in refs[1:-2]:
        total = total + ref[...].astype(F32)
    turned = total.T.astype(BF16)
    refs[-2][...] = turned[0:DIM]
    refs[-1][...] = turned[DIM:]


def finish(parts):
    shape = jax.ShapeDtypeStruct((DIM, PIECE), BF16)
    return pl.pallas_call(
        finish_kernel, out_shape=(shape, shape), in_specs=[VMEM] * len(parts), out_specs=(VMEM, VMEM),
        compiler_params=pltpu.CompilerParams(vmem_limit_bytes=4 * 1024 * 1024),
    )(*parts)


def shift(x, by):
    size = lax.axis_size("ctx")
    pairs = [(i, i + by) for i in range(size) if 0 <= i + by < size]
    return lax.ppermute(x, "ctx", pairs)


def swap(x):
    return lax.ppermute(x, "ctx", [(i, i ^ 1) for i in range(lax.axis_size("ctx"))])


def to_sibling(x, source):
    pairs = [(i, i ^ 1) for i in range(lax.axis_size("ctx")) if i % 2 == source]
    return lax.ppermute(x, "ctx", pairs)


def turn(x, by):
    return lax.ppermute(x, "tp", [(i, (i + by) % 4) for i in range(4)])


def local(queries, key_rows, values, grad_out, doc_ids):
    tp = lax.axis_index("tp")
    odd = lax.rem(lax.axis_index("ctx"), 2) == 1
    q = queries.transpose(1, 2, 0)
    do = grad_out.transpose(1, 2, 0)
    docs = jnp.broadcast_to((doc_ids + 1).astype(BF16)[None], (16, ROWS))
    own = jnp.concatenate([key_rows.T, values.T, docs], axis=0)
    starts = [lax.rem(tp + off, 4) * PIECE for off in OFFSETS]
    half = lax.rem(tp, 2) * HALF
    far_starts = [lax.rem(start + half, ROWS) for start in starts]
    own, starts, far_starts, half, odd = lax.optimization_barrier((own, starts, far_starts, half, odd))
    zero = jnp.zeros((), starts[0].dtype)

    def home_slots(x, starts):
        return [
            lax.dynamic_slice(x, (start, zero), (PIECE, 2 * DIM), allow_negative_indices=False) for start in starts
        ]

    far = shift(lax.dynamic_slice(own, (zero, half), (PACKED, HALF), allow_negative_indices=False), 4)
    near = shift(own, 2)
    far = jnp.concatenate([far, lax.ppermute(far, "tp", [(i, i ^ 1) for i in range(4)])], axis=1)
    own_parts = own_forward(q, own)
    near, far, own_parts = lax.optimization_barrier((near, far, own_parts))
    near_sib = swap(near)
    far_sib = to_sibling(far, 1)
    own_sib = to_sibling(own, 0)
    early_parts = early_forward(near, far, own, own_parts)
    near_sib, far_sib, own_sib, early_parts = lax.optimization_barrier((near_sib, far_sib, own_sib, early_parts))
    parts = middle(do, own, own_parts, early_parts, near_sib, far_sib, own_sib)
    attended, dnear, dnear_sib, near_ds, near_sib_ds, late_w, late_vn, stats = parts[:8]
    back = swap(dnear_sib)
    a1 = (dnear.astype(F32) + back.astype(F32)).astype(BF16)
    a1_here = shift(a1, -2)
    dfar, dsib, far_ds, sib_ds = last(own_parts[1], early_parts, late_w, late_vn, stats, parts[8:])
    back = swap(dsib)
    a2 = (dfar.astype(F32) + jnp.where(odd, back.astype(F32), 0.0)).astype(BF16)
    a2 = home_slots(a2, far_starts)
    a2, stats = lax.optimization_barrier((a2, stats))
    moved = [turn(a2[r], by) for r, by in RETURNS]
    down, _, dq_part = own_back(do, own, own_parts, stats, near, near_sib, near_ds, near_sib_ds)
    moved, down = lax.optimization_barrier((moved, down))
    a2_sum = a2[0].astype(F32)
    for piece in moved:
        a2_sum = a2_sum + piece.astype(F32)
    a2_here = shift(a2_sum.astype(BF16), -4)
    a0 = down.astype(F32) + a1_here.astype(F32) + jnp.where(odd, 0.0, back.astype(F32))
    a0 = home_slots(a0.astype(BF16), starts)
    a0, dq_part = lax.optimization_barrier((a0, dq_part))
    parts = [a0[0], a2_here] + [turn(a0[r], by) for r, by in RETURNS]
    dq = query_grad(dq_part, stats, far, far_sib, own_sib, far_ds, sib_ds)
    dk, dv = finish(parts)
    return attended.transpose(2, 0, 1), dq.transpose(2, 0, 1), dk.T, dv.T


def solution(mesh):
    placed = (P("ctx", "tp", None), P("ctx", None), P("ctx", None), P("ctx", "tp", None), P("ctx"))
    return jax.shard_map(
        local,
        mesh=mesh,
        in_specs=placed,
        out_specs=(
            P("ctx", "tp", None),
            P("ctx", "tp", None),
            P(("ctx", "tp"), None),
            P(("ctx", "tp"), None),
        ),
        check_vma=False,
    )
```

```python
import jax
import jax.numpy as jnp
from jax import lax
from jax.experimental import pallas as pl
from jax.experimental.pallas import tpu as pltpu
from jax.sharding import PartitionSpec as P

LOG2E = 1.4426950408889634
NEGATIVE = -1e30
ROWS = 512
HALF = 256
PIECE = 128
DIM = 192
WIDE = 256
DOC_ROW = 2 * DIM
PACKED = DOC_ROW + 16
HEADS = 3
COLS = HEADS * ROWS
SCALE = DIM ** -0.5
TO_LOG2 = SCALE * LOG2E
OFFSETS = (0, 3, 1, 2)
RETURNS = ((1, -1), (2, 1), (3, 2))
F32 = jnp.float32
BF16 = jnp.bfloat16
VMEM = pl.BlockSpec(memory_space=pltpu.VMEM)
SMEM = pl.BlockSpec(memory_space=pltpu.SMEM)


def dot(a, b):
    return jnp.dot(a, b, preferred_element_type=F32)


def head_cols(head, start=0):
    return slice(head * ROWS + start, (head + 1) * ROWS)


def one_hot(docs, width):
    rows = lax.broadcasted_iota(jnp.int32, (64, width), 0).astype(F32)
    return rows == docs.astype(F32)


def key_features(piece):
    hot = one_hot(piece[DOC_ROW : DOC_ROW + 1, :], piece.shape[1])
    return jnp.concatenate([piece[0:DIM, :], hot.astype(F32).astype(BF16)], axis=0).T


def folded(x):
    return x.reshape(x.shape[0] // 8, 8, x.shape[1])


def spread(row):
    return jnp.broadcast_to(row, (8, row.shape[1]))


def call(kernel, outs, operands, smem, scratch, limit, flops):
    return pl.pallas_call(
        kernel,
        out_shape=tuple(jax.ShapeDtypeStruct(shape, dtype) for shape, dtype in outs),
        in_specs=[SMEM if i in smem else VMEM for i in range(len(operands))],
        out_specs=tuple(SMEM if dtype == jnp.int32 else VMEM for _, dtype in outs),
        scratch_shapes=[pltpu.VMEM(shape, dtype) for shape, dtype in scratch],
        compiler_params=pltpu.CompilerParams(vmem_limit_bytes=limit * 1024 * 1024),
        cost_estimate=pl.CostEstimate(flops=flops, bytes_accessed=8_000_000, transcendentals=1_000_000),
    )(*operands)


def own_kernel(q_ref, own_ref, qe, qn, w_ref, top_ref, total_ref, o_ref):
    docs = own_ref[DOC_ROW : DOC_ROW + 1, :]
    mask_rows = jnp.where(one_hot(docs, ROWS), 0.0, NEGATIVE).astype(BF16)
    kn = key_features(own_ref[...])
    causal = lax.broadcasted_iota(jnp.int32, (HALF, HALF), 0) <= lax.broadcasted_iota(
        jnp.int32, (HALF, HALF), 1
    )
    for head in range(HEADS):
        cols = head_cols(head)
        low = slice(head * ROWS, head * ROWS + HALF)
        high = head_cols(head, HALF)
        qe[0:DIM, cols] = q_ref[head]
        qe[DIM:, cols] = mask_rows
        qn[cols, :] = q_ref[head].T
        s_low = jnp.where(causal, dot(kn[0:HALF], qe[:, low]), NEGATIVE)
        s_high = dot(kn, qe[:, high])
        s_top = s_high[0:HALF]
        s_last = jnp.where(causal, s_high[HALF:], NEGATIVE)
        for span, parts in ((low, (s_low,)), (high, (s_top, s_last))):
            peak = jnp.max(folded(parts[0]), axis=0)
            for s in parts[1:]:
                peak = jnp.maximum(peak, jnp.max(folded(s), axis=0))
            peak = spread(jnp.max(peak, axis=0, keepdims=True) * TO_LOG2)
            top_ref[:, span] = peak
            total = jnp.zeros((8, HALF), F32)
            for part, s in enumerate(parts):
                e = jnp.exp2(folded(s) * TO_LOG2 - peak[None])
                total = total + jnp.sum(e, axis=0)
                w_ref[part * HALF : (part + 1) * HALF, span] = e.reshape(HALF, HALF).astype(BF16)
            total_ref[:, span] = total
        o_ref[:, low] = dot(own_ref[DIM : 2 * DIM, 0:HALF], w_ref[0:HALF, low])
        o_ref[:, high] = dot(own_ref[DIM : 2 * DIM, :], w_ref[:, high])


def own_forward(q, own):
    outs = [
        ((WIDE, COLS), BF16), ((COLS, DIM), BF16), ((ROWS, COLS), BF16),
        ((8, COLS), F32), ((8, COLS), F32), ((DIM, COLS), F32),
    ]
    return call(own_kernel, outs, [q, own], (), [], 8, 800_000_000)


def needed_flag(rows, first_doc):
    matches = jnp.zeros((1, PIECE), F32)
    for row in rows:
        for start in range(0, row.shape[1], PIECE):
            docs = row[:, start : start + PIECE].astype(F32)
            matches = matches + jnp.where(docs == first_doc, 1.0, 0.0)
    return (jnp.max(matches) > 0.0).astype(jnp.int32)


def flag_row(flag):
    return jnp.broadcast_to(flag.astype(F32), (1, COLS))


def read_flag(ref, row):
    return (jnp.max(ref[row : row + 1, 0:PIECE]) > 0.0).astype(jnp.int32)


def whole(tile, flag):
    return (flag, tile, slice(0, ROWS), ROWS)


def far_blocks(tile, flags):
    narrow, low, high = flags
    return [
        (narrow, tile, slice(0, ROWS), HALF),
        (low, tile, slice(0, HALF), ROWS),
        (high, tile, slice(HALF, ROWS), ROWS),
    ]


def block_cols(head, width):
    return slice(head * ROWS, head * ROWS + width)


def score_pass(blocks, kn, vts, qe, scores, w_ref, top0, total0, o0, top, total, o):
    top[...] = top0[...]

    for flag, tile, rows, width in blocks:
        @pl.when(flag > 0)
        def _():
            for head in range(HEADS):
                cols = block_cols(head, width)
                s = dot(kn[tile, rows], qe[:, cols]) * TO_LOG2
                scores[tile, rows, cols] = s
                top[:, cols] = jnp.maximum(top[:, cols], jnp.max(folded(s), axis=0))

    top[...] = spread(jnp.max(top[...], axis=0, keepdims=True))
    shrink = jnp.exp2(top0[...] - top[...])
    total[...] = total0[...] * shrink
    for head in range(HEADS):
        cols = head_cols(head)
        o[:, cols] = o0[:, cols] * shrink[0:1, cols]

    for flag, tile, rows, width in blocks:
        @pl.when(flag > 0)
        def _():
            for head in range(HEADS):
                cols = block_cols(head, width)
                e = jnp.exp2(folded(scores[tile, rows, cols]) - top[:, cols][None])
                total[:, cols] += jnp.sum(e, axis=0)
                w = e.reshape(rows.stop - rows.start, width).astype(BF16)
                w_ref[tile, rows, cols] = w
                o[:, cols] += dot(vts[tile](rows), w)


def prepare(refs, own_ref, kn, vn):
    first_doc = own_ref[DOC_ROW : DOC_ROW + 1, 0:1].astype(F32)
    flags = [needed_flag([ref[DOC_ROW : DOC_ROW + 1, :]], first_doc) for ref in refs]
    for tile, ref in enumerate(refs):
        @pl.when(flags[tile] > 0)
        def _():
            kn[tile] = key_features(ref[...])
            vn[tile] = ref[DIM : 2 * DIM, :].T
    return flags


def early_kernel(
    near_ref, far_ref, own_ref, qe, top0, total0, o0,
    w_ref, vn, top, total, o, flag_ref,
    kn, scores,
):
    refs = (near_ref, far_ref)
    near_flag, far_flag = prepare(refs, own_ref, kn, vn)
    own_docs = own_ref[DOC_ROW : DOC_ROW + 1, :].astype(F32)
    first_doc = own_docs[:, 0:1]
    is_narrow = 1 - needed_flag([own_docs[:, HALF:]], first_doc)
    halves = [needed_flag([far_ref[DOC_ROW : DOC_ROW + 1, span]], first_doc) for span in (slice(0, HALF), slice(HALF, ROWS))]
    far_flags = [far_flag * is_narrow] + [half * (1 - is_narrow) for half in halves]
    for i, flag in enumerate([near_flag] + far_flags):
        flag_ref[i : i + 1, :] = flag_row(flag)
    vts = [lambda rows, ref=ref: ref[DIM : 2 * DIM, rows] for ref in refs]
    score_pass([whole(0, near_flag)] + far_blocks(1, far_flags), kn, vts, qe, scores, w_ref, top0, total0, o0, top, total, o)


def early_forward(near, far, own, own_parts):
    qe, _, _, top, total, o = own_parts
    outs = [
        ((2, ROWS, COLS), BF16), ((2, ROWS, DIM), BF16),
        ((8, COLS), F32), ((8, COLS), F32), ((DIM, COLS), F32), ((8, COLS), F32),
    ]
    scratch = [((2, ROWS, WIDE), BF16), ((2, ROWS, COLS), F32)]
    operands = [near, far, own, qe, top, total, o]
    return call(early_kernel, outs, operands, (), scratch, 12, 3_000_000_000)


def grad_tile(blocks, w, vn, dop, don, delta, qn, ds_ref, out):
    @pl.when(blocks[0][0] == 0)
    def _():
        out[...] = jnp.zeros((ROWS, 2 * DIM), BF16)

    for flag, tile, rows, width in blocks:
        @pl.when(flag > 0)
        def _():
            count = rows.stop - rows.start
            for head in range(HEADS):
                cols = block_cols(head, width)
                dp = folded(dot(vn[tile, rows], dop[:, cols]))
                wide = folded(w[tile, rows, cols].astype(F32))
                ds = (wide * (dp - delta[:, cols][None])).reshape(count, width)
                ds_ref[0, rows, cols] = ds.astype(BF16)
            if width == ROWS:
                dk = dot(ds_ref[0, rows], qn[...])
                dv = dot(w[tile, rows], don[...])
            else:
                spans = [block_cols(head, width) for head in range(HEADS)]
                dk = sum(dot(ds_ref[0, rows, cols], qn[cols, :]) for cols in spans)
                dv = sum(dot(w[tile, rows, cols], don[cols, :]) for cols in spans)
            out[rows] = jnp.concatenate([dk, dv * (1.0 / SCALE)], axis=1).astype(BF16)


def scaled_grads(do_ref, ratio, dop, don):
    for head in range(HEADS):
        cols = head_cols(head)
        scaled = (do_ref[head].astype(F32) * ratio[0:1, cols]).astype(BF16)
        dop[:, cols] = scaled
        don[cols, :] = scaled.T


def middle_kernel(
    early_flag_ref, do_ref, own_ref, qe, qn, top_own, early_w, early_vn, top_early, total_early, o_early,
    near_sib_ref, far_sib_ref, own_sib_ref,
    o_ref, dnear_ref, dnear_sib_ref, near_ds, near_sib_ds, late_w, late_vn, stats, dop_early, don_early, dop, don,
    kn, scores, top, total, o,
):
    refs = (near_sib_ref, far_sib_ref, own_sib_ref)
    late_flags = prepare(refs, own_ref, kn, late_vn)
    early_flags = [read_flag(early_flag_ref, i) for i in range(4)]
    for i, flag in enumerate(early_flags + late_flags):
        stats[48 + i : 49 + i, :] = flag_row(flag)
    vts = [lambda rows, ref=ref: ref[DIM : 2 * DIM, rows] for ref in refs]
    score_pass([whole(tile, flag) for tile, flag in enumerate(late_flags)], kn, vts, qe, scores, late_w, top_early, total_early, o_early, top, total, o)

    early_shrink = jnp.exp2(top_early[...] - top[...])
    own_shrink = jnp.exp2(top_own[...] - top[...])
    for head in range(HEADS):
        cols = head_cols(head)
        inverse = 1.0 / jnp.sum(total[:, cols], axis=0, keepdims=True)
        attended = (o[:, cols] * inverse).astype(BF16)
        o_ref[head] = attended
        delta = jnp.sum(do_ref[head].astype(F32) * attended.astype(F32), axis=0, keepdims=True)
        ratio = spread(inverse * SCALE)
        for i, shrink in enumerate((None, early_shrink, own_shrink)):
            part = ratio if shrink is None else ratio * shrink[:, cols]
            stats[i * 16 : i * 16 + 8, cols] = part
            stats[i * 16 + 8 : i * 16 + 16, cols] = part * delta

    scaled_grads(do_ref, stats.at[16:24], dop_early, don_early)
    scaled_grads(do_ref, stats.at[0:8], dop, don)
    early_delta = stats.at[24:32]
    grad_tile([whole(0, early_flags[0])], early_w, early_vn, dop_early, don_early, early_delta, qn, near_ds, dnear_ref)
    grad_tile([whole(0, late_flags[0])], late_w, late_vn, dop, don, stats.at[8:16], qn, near_sib_ds, dnear_sib_ref)


def middle(do, own, own_parts, early_parts, near_sib, far_sib, own_sib):
    qe, qn, _, top_own, _, _ = own_parts
    early_w, early_vn, top, total, o, flags = early_parts
    outs = [
        ((HEADS, DIM, ROWS), BF16), ((ROWS, 2 * DIM), BF16), ((ROWS, 2 * DIM), BF16),
        ((1, ROWS, COLS), BF16), ((1, ROWS, COLS), BF16),
        ((3, ROWS, COLS), BF16), ((3, ROWS, DIM), BF16), ((56, COLS), F32),
        ((DIM, COLS), BF16), ((COLS, DIM), BF16), ((DIM, COLS), BF16), ((COLS, DIM), BF16),
    ]
    scratch = [
        ((3, ROWS, WIDE), BF16), ((3, ROWS, COLS), F32),
        ((8, COLS), F32), ((8, COLS), F32), ((DIM, COLS), F32),
    ]
    operands = [
        flags, do, own, qe, qn, top_own, early_w, early_vn, top, total, o, near_sib, far_sib, own_sib
    ]
    return call(middle_kernel, outs, operands, (), scratch, 18, 5_000_000_000)


def last_kernel(
    qn, early_w, early_vn, late_w, late_vn, stats, dop_early, don_early, dop, don,
    dfar_ref, dsib_ref, far_ds, sib_ds,
):
    early_delta = stats.at[24:32]
    delta = stats.at[8:16]
    far_flags = [read_flag(stats, 49 + i) for i in range(3)]
    grad_tile(
        far_blocks(1, far_flags), early_w, early_vn, dop_early, don_early, early_delta, qn, far_ds, dfar_ref
    )
    own_sib_flag = read_flag(stats, 54)
    grad_tile([whole(1, read_flag(stats, 53))], late_w, late_vn, dop, don, delta, qn, sib_ds, dsib_ref)

    @pl.when(own_sib_flag > 0)
    def _():
        grad_tile([whole(2, own_sib_flag)], late_w, late_vn, dop, don, delta, qn, sib_ds, dsib_ref)


def last(qn, early_parts, late_w, late_vn, stats, scaled):
    outs = [((ROWS, 2 * DIM), BF16), ((ROWS, 2 * DIM), BF16), ((1, ROWS, COLS), BF16), ((1, ROWS, COLS), BF16)]
    operands = [qn, early_parts[0], early_parts[1], late_w, late_vn, stats, *scaled]
    return call(last_kernel, outs, operands, (), [], 6, 3_000_000_000)


def own_back_kernel(
    do_ref, own_ref, qn, w_ref, stats, near_ref, near_sib_ref, near_ds, near_sib_ds,
    dkv_ref, ds_own, dq_part,
    don,
):
    vn = own_ref[DIM : 2 * DIM, :].T
    for head in range(HEADS):
        cols = head_cols(head)
        low = slice(head * ROWS, head * ROWS + HALF)
        high = head_cols(head, HALF)
        scaled = (do_ref[head].astype(F32) * stats[32:33, cols]).astype(BF16)
        don[cols, :] = scaled.T
        dp_low = dot(vn[0:HALF], scaled[:, 0:HALF])
        dp_high = dot(vn, scaled[:, HALF:])
        ds_own[0:HALF, low] = (w_ref[0:HALF, low].astype(F32) * (dp_low - stats[40:41, low])).astype(BF16)
        ds_own[:, high] = (w_ref[:, high].astype(F32) * (dp_high - stats[40:41, high])).astype(BF16)
    for part in range(2):
        span = slice(part * HALF, (part + 1) * HALF)
        dk = jnp.zeros((HALF, DIM), F32)
        dv = jnp.zeros((HALF, DIM), F32)
        for head in range(HEADS):
            cols = head_cols(head, part * HALF)
            dk = dk + dot(ds_own[span, cols], qn[cols, :])
            dv = dv + dot(w_ref[span, cols], don[cols, :])
        dkv_ref[span, :] = jnp.concatenate([dk, dv * (1.0 / SCALE)], axis=1).astype(BF16)

    for head in range(HEADS):
        low = slice(head * ROWS, head * ROWS + HALF)
        high = head_cols(head, HALF)
        dq_part[:, low] = dot(own_ref[0:DIM, 0:HALF], ds_own[0:HALF, low])
        dq_part[:, high] = dot(own_ref[0:DIM, :], ds_own[:, high])
    query_terms(
        [(whole(0, read_flag(stats, 48)), near_ref, near_ds), (whole(0, read_flag(stats, 52)), near_sib_ref, near_sib_ds)],
        dq_part,
    )


def query_terms(terms, total):
    for (flag, _, rows, width), kt, ds in terms:
        @pl.when(flag > 0)
        def _():
            for head in range(HEADS):
                cols = block_cols(head, width)
                total[:, cols] += dot(kt[0:DIM, rows], ds[0, rows, cols])


def query_grad_kernel(
    dq_part, stats, far_ref, far_sib_ref, own_sib_ref, far_ds, sib_ds,
    dq_ref,
    total,
):
    total[...] = dq_part[...]
    far_flags = [read_flag(stats, 49 + i) for i in range(3)]
    terms = [(block, far_ref, far_ds) for block in far_blocks(0, far_flags)]
    terms.append((whole(0, read_flag(stats, 53)), far_sib_ref, sib_ds))
    terms.append((whole(0, read_flag(stats, 54)), own_sib_ref, sib_ds))
    query_terms(terms, total)
    for head in range(HEADS):
        dq_ref[head] = total[:, head_cols(head)].astype(BF16)


def own_back(do, own, own_parts, stats, near, near_sib, near_ds, near_sib_ds):
    outs = [((ROWS, 2 * DIM), BF16), ((ROWS, COLS), BF16), ((DIM, COLS), F32)]
    operands = [do, own, own_parts[1], own_parts[2], stats, near, near_sib, near_ds, near_sib_ds]
    return call(own_back_kernel, outs, operands, (), [((COLS, DIM), BF16)], 6, 1_000_000_000)


def query_grad(dq_part, stats, far, far_sib, own_sib, far_ds, sib_ds):
    outs = [((HEADS, DIM, ROWS), BF16)]
    operands = [dq_part, stats, far, far_sib, own_sib, far_ds, sib_ds]
    return call(query_grad_kernel, outs, operands, (), [((DIM, COLS), F32)], 6, 1_000_000_000)[0]


def finish_kernel(*refs):
    total = refs[0][...].astype(F32)
    for ref in refs[1:-2]:
        total = total + ref[...].astype(F32)
    turned = total.T.astype(BF16)
    refs[-2][...] = turned[0:DIM]
    refs[-1][...] = turned[DIM:]


def finish(parts):
    shape = jax.ShapeDtypeStruct((DIM, PIECE), BF16)
    return pl.pallas_call(
        finish_kernel, out_shape=(shape, shape), in_specs=[VMEM] * len(parts), out_specs=(VMEM, VMEM),
        compiler_params=pltpu.CompilerParams(vmem_limit_bytes=4 * 1024 * 1024),
    )(*parts)


def shift(x, by):
    size = lax.axis_size("ctx")
    pairs = [(i, i + by) for i in range(size) if 0 <= i + by < size]
    return lax.ppermute(x, "ctx", pairs)


def swap(x):
    return lax.ppermute(x, "ctx", [(i, i ^ 1) for i in range(lax.axis_size("ctx"))])


def to_sibling(x, source):
    pairs = [(i, i ^ 1) for i in range(lax.axis_size("ctx")) if i % 2 == source]
    return lax.ppermute(x, "ctx", pairs)


def turn(x, by):
    return lax.ppermute(x, "tp", [(i, (i + by) % 4) for i in range(4)])


def local(queries, key_rows, values, grad_out, doc_ids):
    tp = lax.axis_index("tp")
    odd = lax.rem(lax.axis_index("ctx"), 2) == 1
    q = queries.transpose(1, 2, 0)
    do = grad_out.transpose(1, 2, 0)
    docs = jnp.broadcast_to((doc_ids + 1).astype(BF16)[None], (16, ROWS))
    own = jnp.concatenate([key_rows.T, values.T, docs], axis=0)
    starts = [lax.rem(tp + off, 4) * PIECE for off in OFFSETS]
    half = lax.rem(tp, 2) * HALF
    far_starts = [lax.rem(start + half, ROWS) for start in starts]
    own, starts, far_starts, half, odd = lax.optimization_barrier((own, starts, far_starts, half, odd))
    zero = jnp.zeros((), starts[0].dtype)

    def home_slots(x, starts):
        return [
            lax.dynamic_slice(x, (start, zero), (PIECE, 2 * DIM), allow_negative_indices=False) for start in starts
        ]

    far = shift(lax.dynamic_slice(own, (zero, half), (PACKED, HALF), allow_negative_indices=False), 4)
    near = shift(own, 2)
    far = jnp.concatenate([far, lax.ppermute(far, "tp", [(i, i ^ 1) for i in range(4)])], axis=1)
    own_parts = own_forward(q, own)
    far_sib = to_sibling(far, 1)
    near, far, own_parts = lax.optimization_barrier((near, far, own_parts))
    near_sib = swap(near)
    own_sib = to_sibling(own, 0)
    early_parts = early_forward(near, far, own, own_parts)
    near_sib, far_sib, own_sib, early_parts = lax.optimization_barrier((near_sib, far_sib, own_sib, early_parts))
    parts = middle(do, own, own_parts, early_parts, near_sib, far_sib, own_sib)
    attended, dnear, dnear_sib, near_ds, near_sib_ds, late_w, late_vn, stats = parts[:8]
    back = swap(dnear_sib)
    a1 = (dnear.astype(F32) + back.astype(F32)).astype(BF16)
    a1_here = shift(a1, -2)
    dfar, dsib, far_ds, sib_ds = last(own_parts[1], early_parts, late_w, late_vn, stats, parts[8:])
    back = swap(dsib)
    a2 = (dfar.astype(F32) + jnp.where(odd, back.astype(F32), 0.0)).astype(BF16)
    a2 = home_slots(a2, far_starts)
    a2, stats = lax.optimization_barrier((a2, stats))
    moved = [turn(a2[r], by) for r, by in RETURNS]
    down, _, dq_part = own_back(do, own, own_parts, stats, near, near_sib, near_ds, near_sib_ds)
    moved, down = lax.optimization_barrier((moved, down))
    a2_sum = a2[0].astype(F32)
    for piece in moved:
        a2_sum = a2_sum + piece.astype(F32)
    a2_here = shift(a2_sum.astype(BF16), -4)
    a0 = down.astype(F32) + a1_here.astype(F32) + jnp.where(odd, 0.0, back.astype(F32))
    a0 = home_slots(a0.astype(BF16), starts)
    a0, dq_part = lax.optimization_barrier((a0, dq_part))
    parts = [a0[0], a2_here] + [turn(a0[r], by) for r, by in RETURNS]
    dq = query_grad(dq_part, stats, far, far_sib, own_sib, far_ds, sib_ds)
    dk, dv = finish(parts)
    return attended.transpose(2, 0, 1), dq.transpose(2, 0, 1), dk.T, dv.T


def solution(mesh):
    placed = (P("ctx", "tp", None), P("ctx", None), P("ctx", None), P("ctx", "tp", None), P("ctx"))
    return jax.shard_map(
        local,
        mesh=mesh,
        in_specs=placed,
        out_specs=(
            P("ctx", "tp", None),
            P("ctx", "tp", None),
            P(("ctx", "tp"), None),
            P(("ctx", "tp"), None),
        ),
        check_vma=False,
    )
```
